256 devices in a mesh: ctx: 16 (over x, z_hi), tp: 16 (over y, z_lo, core).
Axes of the slice: x: 4, y: 4, z: 8 (z_hi: 4, z_lo: 2; z = z_hi * 2 + z_lo), core: 2. Of those that a mesh axis runs over, the one named last changes fastest.
Arguments:
- query_nope: bfloat16 [2048, 8192], P('ctx', 'tp'), may hold values from -12 to 12
- query_rope: bfloat16 [2048, 4096], P('ctx', 'tp'), may hold values from -48 to 48
- latent_cache: bfloat16 [2048, 576], P('ctx'), may hold values from -8 to 8
- up_keys: bfloat16 [512, 8192], P(None, 'tp'), may hold values from -0.25 to 0.25
- up_values: bfloat16 [512, 8192], P(None, 'tp'), may hold values from -0.25 to 0.25
- out_grad: bfloat16 [2048, 8192], P('ctx', 'tp'), may hold values from -6 to 6
- response_mask: int32 [2048], P('ctx'), may hold values 0 or 1
- boundary: int32 [1], replicated, may hold values from 0 to 1023
Outputs:
- attn_out: bfloat16 [2048, 8192], P('ctx', 'tp')
- grad_query_nope: bfloat16 [2048, 8192], P('ctx', 'tp')
- grad_query_rope: bfloat16 [2048, 4096], P('ctx', 'tp')
- grad_latent: float32 [2048, 576], P('ctx')
- grad_up_keys: float32 [512, 8192], P('ctx', 'tp')
- grad_up_values: float32 [512, 8192], P('ctx', 'tp')
The draws below stay inside these ranges and needn't reach their ends.
All inputs are finite; a program needn't handle non-finite values. No bound on the sum of `response_mask` on one device may be relied on, other than what follows from the above.
Results may differ from the reference program's by a relative error of at most 0.03.
Values may be sent and summed in bfloat16 or wider, within the bound.
A program may use at most 64 MiB of HBM per device.

```python
import math
import jax
import jax.numpy as jnp
from jax import lax

HEADS = 64
LATENT = 512
ROPE = 64
NOPE = 128
VDIM = 128
TOK_DEV = 128
SEQ = 2048
N_CTX = 16


def draw_latent_cache(key, part):
    key = jax.random.fold_in(key, 1)
    values = jax.random.normal(key, (SEQ, LATENT + ROPE), jnp.float32)
    return jnp.clip(values, -8.0, 8.0).astype(jnp.bfloat16)


def draw_query_nope(key, part):
    key = jax.random.fold_in(key, 3)
    values = 2.0 * jax.random.normal(key, (SEQ, HEADS * NOPE), jnp.float32)
    return jnp.clip(values, -12.0, 12.0).astype(jnp.bfloat16)


def draw_query_rope(key, part):
    key = jax.random.fold_in(key, 4)
    values = 2.0 * jax.random.normal(key, (SEQ, HEADS * ROPE), jnp.float32)
    return jnp.clip(values, -48.0, 48.0).astype(jnp.bfloat16)


def place_ends(values, rng, low, largest):
    extent = values.shape
    place = [jax.random.randint(jax.random.fold_in(rng, axis), (), 0, extent[axis]) for axis in range(len(extent))]
    values = values.at[tuple(place)].set(low)
    longest = extent.index(max(extent))
    place[longest] = (place[longest] + 1) % extent[longest]
    return values.at[tuple(place)].set(largest)


def steps_of(rng, shape, shards, least, high):
    gain, own = 1.0, jax.random.fold_in(rng, 6)
    for position, parts in shards:
        steps = jnp.exp(jax.random.uniform(jax.random.fold_in(own, position), (parts,), jnp.float32, least / len(shards), high / len(shards)))
        gain = gain * jnp.repeat(steps, shape[position] // parts).reshape([-1 if axis == position else 1 for axis in range(len(shape))])
    return gain


def bell_draw(stream_key, shape, scale, most, pieces=(), held_as=jnp.bfloat16):
    result = scale * jax.random.normal(stream_key, shape, jnp.float32)
    if pieces:
        result = result * steps_of(stream_key, shape, pieces, -0.22, 0.18)
    return jnp.clip(result, -most, most).astype(held_as)


def setup_inputs(seed: int = 0) -> dict:
    keys = jax.random.split(jax.random.key(seed), 9)
    return {
        "query_nope": draw_query_nope(jax.random.fold_in(keys[8], 71), 0),
        "query_rope": draw_query_rope(jax.random.fold_in(keys[8], 71), 0),
        "latent_cache": draw_latent_cache(jax.random.fold_in(keys[8], 71), 0),
        "up_keys": bell_draw(keys[3], (LATENT, HEADS * NOPE), LATENT ** -0.5, 0.25, ((1, 16),)),
        "up_values": bell_draw(keys[4], (LATENT, HEADS * VDIM), LATENT ** -0.5, 0.25, ((1, 16),)),
        "out_grad": bell_draw(keys[5], (SEQ, HEADS * VDIM), 1.0, 6.0, ((0, 16), (1, 16))),
        "response_mask": place_ends((jax.random.randint(keys[6], (SEQ,), 0, 2) < 1).astype(jnp.int32), jax.random.fold_in(keys[6], 1), 0, 1),
        "boundary": jax.random.randint(keys[7], (1,), 0, SEQ // 2).astype(jnp.int32),
    }


def reference(query_nope, query_rope, latent_cache, up_keys, up_values, out_grad, response_mask, boundary):
    scaling = 1.0 / math.sqrt(NOPE + ROPE)
    highest = lax.Precision.HIGHEST
    latent = latent_cache[:, :LATENT]
    rope_keys = latent_cache[:, LATENT:]
    key_nope = jnp.dot(latent, up_keys, preferred_element_type=jnp.float32).astype(jnp.bfloat16)
    value_rows = jnp.dot(latent, up_values, preferred_element_type=jnp.float32).astype(jnp.bfloat16)
    positions = jnp.arange(SEQ, dtype=jnp.int32)
    kept_rows = (response_mask == 1) & (positions >= boundary[0])
    cotangent = jnp.where(kept_rows[:, None], out_grad, jnp.zeros_like(out_grad))

    def heads_first(array, width):
        return jnp.moveaxis(array.reshape(SEQ, HEADS, width), 1, 0)

    def one_head(stacked):
        head_query, head_rope, head_key, head_value, head_grad = stacked
        scores = (jnp.dot(head_query, head_key.T, preferred_element_type=jnp.float32) + jnp.dot(head_rope, rope_keys.T, preferred_element_type=jnp.float32)) * scaling
        row_max = lax.optimization_barrier(jnp.max(scores, axis=1, keepdims=True))
        log_total = row_max + jnp.log(lax.optimization_barrier(jnp.sum(jnp.exp(scores - row_max), axis=1, keepdims=True)))
        probs = jnp.exp(scores - log_total)
        probs_low = probs.astype(jnp.bfloat16)
        head_out = jnp.dot(probs_low, head_value, preferred_element_type=jnp.float32).astype(jnp.bfloat16)
        row_delta = lax.optimization_barrier(jnp.sum(head_grad.astype(jnp.float32) * head_out.astype(jnp.float32), axis=1, keepdims=True))
        prob_grad = jnp.dot(head_grad, head_value.T, preferred_element_type=jnp.float32)
        score_grad = (probs * (prob_grad - row_delta) * scaling).astype(jnp.bfloat16)
        grad_nope = jnp.dot(score_grad, head_key, preferred_element_type=jnp.float32).astype(jnp.bfloat16)
        grad_rope = jnp.dot(score_grad, rope_keys, preferred_element_type=jnp.float32).astype(jnp.bfloat16)
        block_grad = score_grad.astype(jnp.float32).reshape(N_CTX, TOK_DEV, SEQ)
        block_query = head_query.astype(jnp.float32).reshape(N_CTX, TOK_DEV, NOPE)
        key_terms = jnp.einsum('bts,btd->bsd', block_grad, block_query, precision=highest)
        key_grad = lax.optimization_barrier(jnp.sum(lax.optimization_barrier(key_terms.astype(jnp.bfloat16)).astype(jnp.float32), axis=0))
        block_probs = probs_low.astype(jnp.float32).reshape(N_CTX, TOK_DEV, SEQ)
        block_cot = head_grad.astype(jnp.float32).reshape(N_CTX, TOK_DEV, VDIM)
        value_terms = jnp.einsum('bts,btd->bsd', block_probs, block_cot, precision=highest)
        value_grad = lax.optimization_barrier(jnp.sum(lax.optimization_barrier(value_terms.astype(jnp.bfloat16)).astype(jnp.float32), axis=0))
        rope_grad = jnp.dot(score_grad.T, head_rope, preferred_element_type=jnp.float32)
        return (head_out, grad_nope, grad_rope, key_grad, value_grad, rope_grad)
    results = lax.map(one_head, (heads_first(query_nope, NOPE), heads_first(query_rope, ROPE), heads_first(key_nope, NOPE), heads_first(value_rows, VDIM), heads_first(cotangent, VDIM)))

    def rows_first(array):
        return jnp.moveaxis(array, 0, 1).reshape(SEQ, -1)
    attn_out = rows_first(results[0])
    grad_query_nope = rows_first(results[1])
    grad_query_rope = rows_first(results[2])
    key_grad = rows_first(results[3])
    value_grad = rows_first(results[4])
    rope_total = lax.optimization_barrier(jnp.sum(results[5], axis=0))
    latent_part = jnp.dot(key_grad, up_keys.astype(jnp.float32).T, precision=highest) + jnp.dot(value_grad, up_values.astype(jnp.float32).T, precision=highest)
    grad_latent = jnp.concatenate([latent_part, rope_total], axis=1)
    latent_wide = latent.astype(jnp.float32)
    grad_up_keys = jnp.dot(latent_wide.T, key_grad, precision=highest)
    grad_up_values = jnp.dot(latent_wide.T, value_grad, precision=highest)
    return (attn_out, grad_query_nope, grad_query_rope, grad_latent, grad_up_keys, grad_up_values)
```

```python
import math

import jax
import jax.numpy as jnp
from jax import lax
from jax.experimental import pallas as pl
from jax.experimental.pallas import tpu as pltpu
from jax.sharding import PartitionSpec as P

LATENT = 512
ROPE = 64
CACHE = LATENT + ROPE
NOPE = 128
VDIM = 128
ROWS = 128
HEADS = 4
SEQ = 2048
T = HEADS * ROWS
SCALE = 1.0 / math.sqrt(NOPE + ROPE)
LN2 = math.log(2.0)
TO_BASE2 = SCALE / LN2
MESH = pl.DeviceIdType.MESH
BF16 = jnp.bfloat16
F32 = jnp.float32
N_SEMS = 112


def dot(a, b):
    return jnp.dot(a, b, preferred_element_type=F32)


def dot_nt(a, b):
    return lax.dot_general(a, b, (((1,), (1,)), ((), ())), preferred_element_type=F32)


def dot_tn(a, b):
    return lax.dot_general(a, b, (((0,), (0,)), ((), ())), preferred_element_type=F32)


def kernel(
    qn_in, qr_in, lc_in, wk_in, wv_in, og_in, mask_ref, bound_ref,
    out_ref, gqn_ref, gqr_ref, glat_ref, gwk_ref, gwv_ref,
    qn, qr, wk, wv, og, cot, cache, cache_t, q_rows, q_cols,
    e_buf, dp_buf, m_run, l_run, d_run, m_at, ds_p, acc, og_t,
    d_buf, d_recv, a_buf, y_buf, y_out, a2_buf, x_recv, a3_buf, z_recv, gather,
    w_buf, w_ring, w_out, w2_buf, w_recv,
    in_sems, send_sems, recv_sems,
):
    ctx, tp = lax.axis_index("ctx"), lax.axis_index("tp")
    x, zh = ctx // 4, ctx % 4
    y, zl, core = tp // 4, (tp // 2) % 2, tp % 2

    def dev(dx=0, zh_to=None, y_to=None, zl_to=None, core_to=None):
        to_x = (x + dx) % 4
        to_zh = zh if zh_to is None else zh_to
        to_y = y if y_to is None else y_to
        to_zl = zl if zl_to is None else zl_to
        to_core = core if core_to is None else core_to
        return (to_x * 4 + to_zh, to_y * 4 + to_zl * 2 + to_core)

    counter = [0]
    sent = []

    def new_sem():
        counter[0] += 1
        return counter[0] - 1

    def send(src, dst, sem, to):
        copy = pltpu.make_async_remote_copy(
            src_ref=src, dst_ref=dst, send_sem=send_sems.at[sem], recv_sem=recv_sems.at[sem],
            device_id=to, device_id_type=MESH,
        )
        copy.start()
        sent.append(copy)

    def arrived(dst, sem):
        pltpu.make_async_remote_copy(
            src_ref=dst, dst_ref=dst, send_sem=send_sems.at[sem], recv_sem=recv_sems.at[sem],
            device_id=dev(), device_id_type=MESH,
        ).wait_recv()

    own_rows = pl.ds(pl.multiple_of(ctx * ROWS, ROWS), ROWS)
    loads = [
        pltpu.make_async_copy(src, dst, in_sems.at[i])
        for i, (src, dst) in enumerate(
            [(lc_in, cache.at[own_rows, :]), (qn_in, qn), (wk_in, wk), (og_in, og), (wv_in, wv), (qr_in, qr)]
        )
    ]
    for load in loads:
        load.start()
    z_at = zh * 2 + zl
    partner = dev(core_to=1 - core)
    z_peers = [((z_at + d) % 8) for d in range(1, 8)]
    z_devs = [dev(zh_to=z // 2, zl_to=z % 2) for z in z_peers]
    x_devs = [dev(dx=d) for d in range(1, 4)]
    y_devs = [dev(y_to=(y + d) % 4) for d in range(1, 4)]
    yc_devs = [dev(y_to=(y + d) % 4, core_to=1 - core) for d in range(1, 4)]
    barrier = pltpu.get_barrier_semaphore()
    peers = [partner] + z_devs + x_devs + y_devs + yc_devs
    for peer in peers:
        pl.semaphore_signal(barrier, inc=1, device_id=peer, device_id_type=MESH)
    pl.semaphore_wait(barrier, len(peers))
    loads[0].wait()

    outward = zl * 2 - 1
    out_dev = dev(zh_to=(zh + outward + 4) % 4, zl_to=1 - zl)
    in_dev = dev(zl_to=1 - zl)
    zh_of = [zh, (zh + outward + 4) % 4, (zh - outward + 4) % 4, (zh + 2) % 4]

    def chunk(dx, j, half, start=0, rows=64):
        block = ((x + dx) % 4) * 4 + zh_of[j]
        return cache.at[pl.ds(pl.multiple_of(block * ROWS + half * 64 + start, 16), rows), :]

    z_sem = [new_sem() for _ in range(4)]
    xm_sem = [new_sem() for _ in range(4)]
    xp_sem = [new_sem() for _ in range(4)]
    rm_sem = [new_sem() for _ in range(4)]
    rp_sem = [new_sem() for _ in range(4)]
    core_sem = [[new_sem() for _ in range(4)] for _ in range(4)]

    def to_core(dx, j):
        send(chunk(dx, j, core), chunk(dx, j, core), core_sem[dx][j], partner)

    def from_core(dx, j):
        arrived(chunk(dx, j, 1 - core), core_sem[dx][j])

    def along_x(j):
        send(chunk(0, j, core), chunk(0, j, core), xm_sem[j], x_devs[0])
        send(chunk(0, j, core), chunk(0, j, core), xp_sem[j], x_devs[2])

    def relay_x(j):
        arrived(chunk(3, j, core), xm_sem[j])
        send(chunk(3, j, core, 0, 32), chunk(3, j, core, 0, 32), rm_sem[j], x_devs[0])
        to_core(3, j)
        arrived(chunk(1, j, core), xp_sem[j])
        send(chunk(1, j, core, 32, 32), chunk(1, j, core, 32, 32), rp_sem[j], x_devs[2])
        to_core(1, j)

    def far_x(j):
        arrived(chunk(2, j, core, 0, 32), rm_sem[j])
        arrived(chunk(2, j, core, 32, 32), rp_sem[j])
        to_core(2, j)

    send(chunk(0, 0, core), chunk(0, 0, core), z_sem[1], out_dev)
    along_x(0)

    for load in loads[1:]:
        load.wait()
    position = ctx * ROWS + lax.broadcasted_iota(jnp.int32, (1, ROWS), 1)
    kept = (mask_ref[...] == 1) & (position >= bound_ref[0])
    diagonal = lax.broadcasted_iota(jnp.int32, (ROWS, ROWS), 0) == lax.broadcasted_iota(
        jnp.int32, (ROWS, ROWS), 1
    )
    keep = jnp.where(diagonal & kept, 1.0, 0.0).astype(BF16)
    cot[...] = dot(keep, og[...]).astype(BF16)
    eye = (
        lax.broadcasted_iota(jnp.int32, (ROPE, ROPE), 0)
        == lax.broadcasted_iota(jnp.int32, (ROPE, ROPE), 1)
    ).astype(F32).astype(BF16)
    q_rows[T:, LATENT:] = jnp.zeros((T, ROPE), BF16)
    for h in range(HEADS):
        cols = slice(h * 128, (h + 1) * 128)
        low = slice(T + h * 128, T + (h + 1) * 128)
        q_rows[cols, :LATENT] = (dot_nt(qn[:, cols], wk[:, cols]) * TO_BASE2).astype(BF16)
        q_cols[:LATENT, cols] = (dot_nt(wk[:, cols], qn[:, cols]) * TO_BASE2).astype(BF16)
        rope = (qr[:, h * ROPE:(h + 1) * ROPE].astype(F32) * TO_BASE2).astype(BF16)
        q_rows[cols, LATENT:] = rope
        q_cols[LATENT:, cols] = dot_nt(eye, rope).astype(BF16)
        q_rows[low, :LATENT] = dot_nt(cot[:, cols], wv[:, cols]).astype(BF16)
        q_cols[:LATENT, low] = dot_nt(wv[:, cols], cot[:, cols]).astype(BF16)

    def group(dx, first):
        g = (x + dx) % 4
        rows = pl.ds(pl.multiple_of(g * 512, 512), 512)

        def columns(c, carry):
            s_cols = pl.ds(pl.multiple_of(c * 256, 256), 256)
            p_cols = pl.ds(pl.multiple_of(T + c * 256, 256), 256)
            s = dot(cache[rows, :], q_cols[:, s_cols])
            dp = dot(cache[rows, :LATENT], q_cols[:LATENT, p_cols])
            dp_buf[rows, s_cols] = dp
            top = jnp.max(s, axis=0, keepdims=True)
            if not first:
                top = jnp.maximum(top, m_run[:, s_cols])
            e = jnp.exp2(s - top)
            e_buf[rows, s_cols] = e
            total = jnp.sum(e, axis=0, keepdims=True)
            weighted = jnp.sum(e * dp, axis=0, keepdims=True)
            if not first:
                shrink = jnp.exp2(m_run[:, s_cols] - top)
                total = total + l_run[:, s_cols] * shrink
                weighted = weighted + d_run[:, s_cols] * shrink
            m_run[:, s_cols] = top
            l_run[:, s_cols] = total
            d_run[:, s_cols] = weighted
            m_at[g, :, s_cols] = top
            return carry

        lax.fori_loop(0, 2, columns, 0)
        cache_t[:LATENT, rows] = cache[rows, :LATENT].T
        cache_t[LATENT:, rows] = dot_nt(eye, cache[rows, LATENT:]).astype(BF16)

    arrived(chunk(0, 1, core), z_sem[1])
    send(chunk(0, 1, core), chunk(0, 1, core), z_sem[2], in_dev)
    along_x(1)
    to_core(0, 1)
    arrived(chunk(0, 2, core), z_sem[2])
    send(chunk(0, 2, core), chunk(0, 2, core), z_sem[3], out_dev)
    along_x(2)
    to_core(0, 2)
    relay_x(0)
    arrived(chunk(0, 3, core), z_sem[3])
    along_x(3)
    to_core(0, 3)
    relay_x(1)
    for j in range(1, 4):
        from_core(0, j)
    group(0, True)
    relay_x(2)
    relay_x(3)
    far_x(0)
    far_x(1)
    for j in range(4):
        from_core(1, j)
    group(1, False)
    far_x(2)
    for j in range(4):
        from_core(3, j)
    group(3, False)
    far_x(3)
    for j in range(4):
        from_core(2, j)
    group(2, False)

    l_run[...] = 1.0 / l_run[...]
    d_run[...] = d_run[...] * l_run[...]
    d_sem = [new_sem() for _ in range(4)]

    def finish(g):
        rows = slice(g * 512, (g + 1) * 512)

        def piece(i, carry):
            part = pl.ds(pl.multiple_of(g * 512 + i * 64, 64), 64)
            weight = jnp.exp2(m_at[g] - m_run[...]) * l_run[...]
            p = e_buf[part, :] * weight
            ds_p[part, T:] = p.astype(BF16)
            ds_p[part, :T] = (p * (dp_buf[part, :] - d_run[...]) * LN2).astype(BF16)
            return carry

        lax.fori_loop(0, 8, piece, 0)
        terms = dot(ds_p[rows, :], q_rows[...])
        d_buf[g * 4:(g + 1) * 4] = terms.astype(BF16).reshape(4, ROWS, CACHE)
        send(
            d_buf.at[pl.ds(g * 4, 4), pl.ds(pl.multiple_of((1 - core) * 64, 64), 64), :],
            d_recv.at[pl.ds(g * 4, 4)], d_sem[g], partner,
        )

    def pair_sum(g):
        arrived(d_recv.at[pl.ds(g * 4, 4)], d_sem[g])

        def block(b, carry):
            own = d_buf[b, pl.ds(pl.multiple_of(core * 64, 64), 64), :]
            a_buf[b] = (own.astype(F32) + d_recv[b].astype(F32)).astype(BF16)
            return carry

        lax.fori_loop(g * 4, g * 4 + 4, block, 0)

    y_sem = [new_sem() for _ in range(6)]

    def y_rows(d):
        return pl.ds(pl.multiple_of(((y + d) % 4) * 16, 16), 16)

    lower, upper = pl.ds(0, 8), pl.ds(8, 8)
    finish(0)
    finish(1)
    pair_sum(0)
    finish(2)
    pair_sum(1)
    send(a_buf.at[lower, y_rows(2), :], y_buf.at[0], y_sem[0], y_devs[0])
    send(a_buf.at[lower, y_rows(3), :], y_buf.at[2], y_sem[2], y_devs[2])
    finish(3)
    pair_sum(2)
    pair_sum(3)
    send(a_buf.at[upper, y_rows(2), :], y_buf.at[1], y_sem[1], y_devs[2])
    send(a_buf.at[upper, y_rows(1), :], y_buf.at[3], y_sem[3], y_devs[0])

    def latent_out(c, carry):
        cols = pl.ds(pl.multiple_of(c * 256, 256), 256)
        part = dot(cache_t[...], ds_p[:, cols])
        acc[:, cols] = part
        og_t[:, cols] = part.astype(BF16)
        return carry

    lax.fori_loop(0, 4, latent_out, 0)

    for h in range(HEADS):
        cols = slice(h * 128, (h + 1) * 128)
        low = slice(T + h * 128, T + (h + 1) * 128)
        w_buf[0, :, :, cols] = (dot(og_t[:LATENT, cols], qn[:, cols]) * TO_BASE2).astype(BF16).reshape(4, 128, 128)
        w_buf[1, :, :, cols] = dot(og_t[:LATENT, low], cot[:, cols]).astype(BF16).reshape(4, 128, 128)
    wx_sem = [new_sem() for _ in range(6)]

    def at_x(d):
        return (x + d) % 4

    send(w_buf.at[0, at_x(2)], w_ring.at[0], wx_sem[0], x_devs[0])
    send(w_buf.at[1, at_x(2)], w_ring.at[1], wx_sem[1], x_devs[2])
    send(w_buf.at[0, at_x(3)], w_ring.at[2], wx_sem[2], x_devs[2])
    send(w_buf.at[1, at_x(1)], w_ring.at[3], wx_sem[3], x_devs[0])

    for h in range(HEADS):
        cols = slice(h * 128, (h + 1) * 128)
        low = slice(T + h * 128, T + (h + 1) * 128)
        out_ref[:, cols] = dot_tn(og_t[:LATENT, low], wv[:, cols]).astype(BF16)
        gqn_ref[:, cols] = (dot_tn(og_t[:LATENT, cols], wk[:, cols]) * TO_BASE2).astype(BF16)
        gqr_ref[:, h * ROPE:(h + 1) * ROPE] = (acc[LATENT:, cols].T * TO_BASE2).astype(BF16)

    def y_combine(slot, base, d):
        def block(b, carry):
            own = a_buf[base + b, y_rows(d), :]
            y_out[slot, b] = (own.astype(F32) + y_buf[slot, b].astype(F32)).astype(BF16)
            return carry

        lax.fori_loop(0, 8, block, 0)

    arrived(y_buf.at[0], y_sem[0])
    y_combine(0, 0, 1)
    send(y_out.at[0], y_buf.at[4], y_sem[4], y_devs[0])
    arrived(y_buf.at[1], y_sem[1])
    y_combine(1, 8, 3)
    send(y_out.at[1], y_buf.at[5], y_sem[5], y_devs[2])

    arrived(w_ring.at[0], wx_sem[0])
    w_out[0] = (w_buf[0, at_x(1)].astype(F32) + w_ring[0].astype(F32)).astype(BF16)
    send(w_out.at[0], w_ring.at[4], wx_sem[4], x_devs[0])
    arrived(w_ring.at[1], wx_sem[1])
    w_out[1] = (w_buf[1, at_x(3)].astype(F32) + w_ring[1].astype(F32)).astype(BF16)
    send(w_out.at[1], w_ring.at[5], wx_sem[5], x_devs[2])

    for slot, sem in ((2, 2), (3, 3), (4, 4), (5, 5)):
        arrived(y_buf.at[slot], y_sem[sem])

    def y_sum(b, carry):
        first = a_buf[b, y_rows(0), :].astype(F32) + y_buf[2, b].astype(F32) + y_buf[4, b].astype(F32)
        a2_buf[b] = first.astype(BF16)
        second = a_buf[8 + b, y_rows(0), :].astype(F32) + y_buf[3, b].astype(F32) + y_buf[5, b].astype(F32)
        a2_buf[8 + b] = second.astype(BF16)
        return carry

    lax.fori_loop(0, 8, y_sum, 0)
    x_sem = [new_sem() for _ in range(3)]
    for d in range(1, 4):
        send(a2_buf.at[pl.ds(pl.multiple_of(at_x(d) * 4, 4), 4)], x_recv.at[d - 1], x_sem[d - 1], x_devs[d - 1])

    for slot, sem in ((2, 2), (3, 3), (4, 4), (5, 5)):
        arrived(w_ring.at[slot], wx_sem[sem])
    w2_buf[0] = (w_buf[0, x].astype(F32) + w_ring[2].astype(F32) + w_ring[4].astype(F32)).astype(BF16)
    w2_buf[1] = (w_buf[1, x].astype(F32) + w_ring[3].astype(F32) + w_ring[5].astype(F32)).astype(BF16)
    wz_sem = [new_sem() for _ in range(3)]

    def w_rows(d):
        return pl.ds(pl.multiple_of(((zh + d) % 4) * 32, 32), 32)

    for d in range(1, 4):
        send(w2_buf.at[:, w_rows(d), :], w_recv.at[d - 1], wz_sem[d - 1], dev(zh_to=(zh + d) % 4))

    for d in range(3):
        arrived(x_recv.at[d], x_sem[d])
    for b in range(4):
        total = a2_buf[x * 4 + b].astype(F32)
        for d in range(3):
            total = total + x_recv[d, b].astype(F32)
        a3_buf[b] = total.astype(BF16)
    zz_sem = [new_sem() for _ in range(7)]
    for d in range(7):
        send(a3_buf.at[z_peers[d] // 2], z_recv.at[d], zz_sem[d], z_devs[d])

    for d in range(3):
        arrived(w_recv.at[d], wz_sem[d])
    for kind, ref in ((0, gwk_ref), (1, gwv_ref)):
        total = w2_buf[kind, w_rows(0), :].astype(F32)
        for d in range(3):
            total = total + w_recv[d, kind].astype(F32)
        ref[...] = total

    for d in range(7):
        arrived(z_recv.at[d], zz_sem[d])
    total = a3_buf[zh].astype(F32)
    for d in range(7):
        total = total + z_recv[d].astype(F32)

    def share(dy, other):
        half = 1 - core if other else core
        return gather.at[pl.ds(pl.multiple_of(half * 64 + ((y + dy) % 4) * 16, 16), 16), :]

    mine = share(0, False)
    mine[...] = total.astype(BF16)
    g_sem = [[new_sem() for _ in range(4)] for _ in range(2)]
    send(mine, mine, g_sem[1][0], partner)
    for d in range(1, 4):
        send(mine, mine, g_sem[0][d], y_devs[d - 1])
        send(mine, mine, g_sem[1][d], yc_devs[d - 1])
    arrived(share(0, True), g_sem[1][0])
    for d in range(1, 4):
        arrived(share(4 - d, False), g_sem[0][d])
        arrived(share(4 - d, True), g_sem[1][d])
    glat_ref[...] = gather[...].astype(F32)
    for copy in sent:
        copy.wait_send()
    assert counter[0] <= N_SEMS


def per_device(
    query_nope, query_rope, latent_cache, up_keys, up_values, out_grad, response_mask, boundary
):
    anywhere = pl.BlockSpec(memory_space=pl.ANY)
    vmem = pl.BlockSpec(memory_space=pltpu.VMEM)
    scratch = [
        ((ROWS, T), BF16), ((ROWS, HEADS * ROPE), BF16), ((LATENT, T), BF16), ((LATENT, T), BF16),
        ((ROWS, T), BF16), ((ROWS, T), BF16),
        ((SEQ, CACHE), BF16), ((CACHE, SEQ), BF16),
        ((2 * T, CACHE), BF16), ((CACHE, 2 * T), BF16),
        ((SEQ, T), F32), ((SEQ, T), F32),
        ((1, T), F32), ((1, T), F32), ((1, T), F32), ((4, 1, T), F32),
        ((SEQ, 2 * T), BF16),
        ((CACHE, 2 * T), F32), ((CACHE, 2 * T), BF16),
        ((16, ROWS, CACHE), BF16), ((16, 64, CACHE), BF16), ((16, 64, CACHE), BF16),
        ((6, 8, 16, CACHE), BF16), ((2, 8, 16, CACHE), BF16), ((16, 16, CACHE), BF16),
        ((3, 4, 16, CACHE), BF16), ((4, 16, CACHE), BF16), ((7, 16, CACHE), BF16), ((ROWS, CACHE), BF16),
        ((2, 4, 128, T), BF16), ((6, 128, T), BF16), ((2, 128, T), BF16),
        ((2, 128, T), BF16), ((3, 2, 32, T), BF16),
    ]
    return pl.pallas_call(
        kernel,
        out_shape=(
            jax.ShapeDtypeStruct((ROWS, HEADS * VDIM), BF16),
            jax.ShapeDtypeStruct((ROWS, HEADS * NOPE), BF16),
            jax.ShapeDtypeStruct((ROWS, HEADS * ROPE), BF16),
            jax.ShapeDtypeStruct((ROWS, CACHE), F32),
            jax.ShapeDtypeStruct((32, HEADS * NOPE), F32),
            jax.ShapeDtypeStruct((32, HEADS * VDIM), F32),
        ),
        in_specs=[anywhere] * 6 + [vmem, pl.BlockSpec(memory_space=pltpu.SMEM)],
        out_specs=(vmem,) * 6,
        scratch_shapes=[pltpu.VMEM(shape, dtype) for shape, dtype in scratch]
        + [
            pltpu.SemaphoreType.DMA((6,)),
            pltpu.SemaphoreType.DMA((N_SEMS,)),
            pltpu.SemaphoreType.DMA((N_SEMS,)),
        ],
        compiler_params=pltpu.CompilerParams(
            collective_id=0, has_side_effects=True, vmem_limit_bytes=56 * 1024 * 1024
        ),
        cost_estimate=pl.CostEstimate(flops=8 * 10**9, bytes_accessed=4 * 10**6, transcendentals=10**6),
    )(
        query_nope, query_rope, latent_cache, up_keys, up_values, out_grad,
        response_mask.reshape(1, ROWS), boundary,
    )


def solution(mesh):
    in_specs = (
        P("ctx", "tp"),
        P("ctx", "tp"),
        P("ctx", None),
        P(None, "tp"),
        P(None, "tp"),
        P("ctx", "tp"),
        P("ctx"),
        P(),
    )
    out_specs = (
        P("ctx", "tp"),
        P("ctx", "tp"),
        P("ctx", "tp"),
        P("ctx", None),
        P("ctx", "tp"),
        P("ctx", "tp"),
    )
    return jax.shard_map(
        per_device, mesh=mesh, in_specs=in_specs, out_specs=out_specs, check_vma=False
    )
```

```python
import math

import jax
import jax.numpy as jnp
from jax import lax
from jax.experimental import pallas as pl
from jax.experimental.pallas import tpu as pltpu
from jax.sharding import PartitionSpec as P

LATENT = 512
ROPE = 64
CACHE = LATENT + ROPE
NOPE = 128
VDIM = 128
ROWS = 128
HEADS = 4
SEQ = 2048
T = HEADS * ROWS
SCALE = 1.0 / math.sqrt(NOPE + ROPE)
LN2 = math.log(2.0)
TO_BASE2 = SCALE / LN2
MESH = pl.DeviceIdType.MESH
BF16 = jnp.bfloat16
F32 = jnp.float32
N_SEMS = 160


def dot(a, b):
    return jnp.dot(a, b, preferred_element_type=F32)


def dot_nt(a, b):
    return lax.dot_general(a, b, (((1,), (1,)), ((), ())), preferred_element_type=F32)


def dot_tn(a, b):
    return lax.dot_general(a, b, (((0,), (0,)), ((), ())), preferred_element_type=F32)


def kernel(
    qn_in, qr_in, lc_in, wk_in, wv_in, og_in, mask_ref, bound_ref,
    out_to, gqn_to, gqr_to, glat_to, gwk_to, gwv_to,
    lc, qn, qr, wk, wv, og, cot, cache, cache_t, q_rows, q_cols,
    e_buf, dp_buf, m_run, l_run, d_run, m_at, ds_p, acc, og_t,
    d_buf, d_recv, a_buf, y_buf, y_out, a2_buf, x_recv, a3_buf, z_recv, gather,
    w_buf, w_ring, w_out, w2_buf, w_recv,
    out_ref, gqn_ref, gqr_ref, gwk_ref, gwv_ref,
    in_sems, out_sems, send_sems, recv_sems,
):
    ctx, tp = lax.axis_index("ctx"), lax.axis_index("tp")
    x, zh = ctx // 4, ctx % 4
    y, zl, core = tp // 4, (tp // 2) % 2, tp % 2
    parity = y % 2

    def dev(dx=0, zh_to=None, y_to=None, zl_to=None, core_to=None):
        to_x = (x + dx) % 4
        to_zh = zh if zh_to is None else zh_to
        to_y = y if y_to is None else y_to
        to_zl = zl if zl_to is None else zl_to
        to_core = core if core_to is None else core_to
        return (to_x * 4 + to_zh, to_y * 4 + to_zl * 2 + to_core)

    counter = [0]
    sent = []

    def new_sem():
        counter[0] += 1
        return counter[0] - 1

    def send(src, dst, sem, to):
        copy = pltpu.make_async_remote_copy(
            src_ref=src, dst_ref=dst, send_sem=send_sems.at[sem], recv_sem=recv_sems.at[sem],
            device_id=to, device_id_type=MESH,
        )
        copy.start()
        sent.append(copy)

    def arrived(dst, sem):
        pltpu.make_async_remote_copy(
            src_ref=dst, dst_ref=dst, send_sem=send_sems.at[sem], recv_sem=recv_sems.at[sem],
            device_id=dev(), device_id_type=MESH,
        ).wait_recv()

    own_rows = pl.ds(pl.multiple_of(ctx * ROWS, ROWS), ROWS)
    loads = [
        pltpu.make_async_copy(src, dst, in_sems.at[i])
        for i, (src, dst) in enumerate(
            [(lc_in, lc), (qn_in, qn), (wk_in, wk), (og_in, og), (wv_in, wv), (qr_in, qr)]
        )
    ]
    for load in loads:
        load.start()
    z_at = zh * 2 + zl
    partner = dev(core_to=1 - core)
    z_peers = [((z_at + d) % 8) for d in range(1, 8)]
    z_devs = [dev(zh_to=z // 2, zl_to=z % 2) for z in z_peers]
    x_devs = [dev(dx=d) for d in range(1, 4)]
    y_devs = [dev(y_to=(y + d) % 4) for d in range(1, 4)]
    yc_devs = [dev(y_to=(y + d) % 4, core_to=1 - core) for d in range(1, 4)]
    barrier = pltpu.get_barrier_semaphore()
    peers = [partner] + z_devs + x_devs + y_devs + yc_devs
    for peer in peers:
        pl.semaphore_signal(barrier, inc=1, device_id=peer, device_id_type=MESH)
    loads[0].wait()
    whole = (
        lax.broadcasted_iota(jnp.int32, (ROWS, ROWS), 0) == lax.broadcasted_iota(jnp.int32, (ROWS, ROWS), 1)
    ).astype(F32).astype(BF16)
    cache[own_rows, :] = dot_nt(whole, lc[...]).astype(BF16)
    pl.semaphore_wait(barrier, len(peers))

    zh_of = [zh, (zh + 1) % 4, (zh + 3) % 4, (zh + 2) % 4]
    own_start = core * 64 + parity * 32
    mate_start = core * 64 + (1 - parity) * 32

    def chunk(dx, j, start, rows=32):
        block = ((x + dx) % 4) * 4 + zh_of[j]
        return cache.at[pl.ds(pl.multiple_of(block * ROWS + start, 16), rows), :]

    z_sem = [new_sem() for _ in range(4)]
    xm_sem = [new_sem() for _ in range(4)]
    xp_sem = [new_sem() for _ in range(4)]
    rm_sem = [new_sem() for _ in range(4)]
    rp_sem = [new_sem() for _ in range(4)]
    ym_sem = [[new_sem() for _ in range(4)] for _ in range(4)]
    yp_sem = [[new_sem() for _ in range(4)] for _ in range(4)]
    core_sem = [[new_sem() for _ in range(4)] for _ in range(4)]
    mate_sem = [[new_sem() for _ in range(4)] for _ in range(4)]

    def same(ref, sem, to):
        send(ref, ref, sem, to)

    def share(dx, j):
        same(chunk(dx, j, own_start, 16), ym_sem[dx][j], y_devs[0])
        same(chunk(dx, j, own_start + 16, 16), yp_sem[dx][j], y_devs[2])
        same(chunk(dx, j, own_start), core_sem[dx][j], partner)

    def from_y(dx, j):
        arrived(chunk(dx, j, mate_start, 16), ym_sem[dx][j])
        arrived(chunk(dx, j, mate_start + 16, 16), yp_sem[dx][j])
        same(chunk(dx, j, mate_start), mate_sem[dx][j], partner)

    def from_core(dx, j):
        arrived(chunk(dx, j, (1 - core) * 64 + parity * 32), core_sem[dx][j])
        arrived(chunk(dx, j, (1 - core) * 64 + (1 - parity) * 32), mate_sem[dx][j])

    def along_x(j):
        same(chunk(0, j, own_start), xm_sem[j], x_devs[0])
        same(chunk(0, j, own_start), xp_sem[j], x_devs[2])

    def from_z(j):
        arrived(chunk(0, j, own_start), z_sem[j])
        along_x(j)
        share(0, j)

    def from_x(j):
        arrived(chunk(3, j, own_start), xm_sem[j])
        same(chunk(3, j, own_start, 16), rm_sem[j], x_devs[0])
        share(3, j)
        arrived(chunk(1, j, own_start), xp_sem[j])
        same(chunk(1, j, own_start + 16, 16), rp_sem[j], x_devs[2])
        share(1, j)

    def from_far(j):
        arrived(chunk(2, j, own_start, 16), rm_sem[j])
        arrived(chunk(2, j, own_start + 16, 16), rp_sem[j])
        share(2, j)

    same(chunk(0, 0, own_start), z_sem[2], dev(zh_to=zh_of[1]))
    same(chunk(0, 0, own_start), z_sem[1], dev(zh_to=zh_of[2]))
    along_x(0)
    same(chunk(0, 0, own_start), z_sem[3], dev(zh_to=zh_of[3]))

    for load in loads[1:]:
        load.wait()
    position = ctx * ROWS + lax.broadcasted_iota(jnp.int32, (1, ROWS), 1)
    kept = (mask_ref[...] == 1) & (position >= bound_ref[0])
    diagonal = lax.broadcasted_iota(jnp.int32, (ROWS, ROWS), 0) == lax.broadcasted_iota(
        jnp.int32, (ROWS, ROWS), 1
    )
    keep = jnp.where(diagonal & kept, 1.0, 0.0).astype(BF16)
    cot[...] = dot(keep, og[...]).astype(BF16)
    eye = (
        lax.broadcasted_iota(jnp.int32, (ROPE, ROPE), 0)
        == lax.broadcasted_iota(jnp.int32, (ROPE, ROPE), 1)
    ).astype(F32).astype(BF16)
    q_rows[T:, LATENT:] = jnp.zeros((T, ROPE), BF16)
    def products(h):
        cols = slice(h * 128, (h + 1) * 128)
        low = slice(T + h * 128, T + (h + 1) * 128)
        q_rows[cols, :LATENT] = (dot_nt(qn[:, cols], wk[:, cols]) * TO_BASE2).astype(BF16)
        q_cols[:LATENT, cols] = (dot_nt(wk[:, cols], qn[:, cols]) * TO_BASE2).astype(BF16)
        rope = (qr[:, h * ROPE:(h + 1) * ROPE].astype(F32) * TO_BASE2).astype(BF16)
        q_rows[cols, LATENT:] = rope
        q_cols[LATENT:, cols] = dot_nt(eye, rope).astype(BF16)
        q_rows[low, :LATENT] = dot_nt(cot[:, cols], wv[:, cols]).astype(BF16)
        q_cols[:LATENT, low] = dot_nt(wv[:, cols], cot[:, cols]).astype(BF16)

    def group(dx, first):
        g = (x + dx) % 4
        rows = pl.ds(pl.multiple_of(g * 512, 512), 512)

        def columns(c, carry):
            s_cols = pl.ds(pl.multiple_of(c * 256, 256), 256)
            p_cols = pl.ds(pl.multiple_of(T + c * 256, 256), 256)
            s = dot(cache[rows, :], q_cols[:, s_cols])
            dp = dot(cache[rows, :LATENT], q_cols[:LATENT, p_cols])
            dp_buf[rows, s_cols] = dp
            top = jnp.max(s, axis=0, keepdims=True)
            if not first:
                top = jnp.maximum(top, m_run[:, s_cols])
            e = jnp.exp2(s - top)
            e_buf[rows, s_cols] = e
            total = jnp.sum(e, axis=0, keepdims=True)
            weighted = jnp.sum(e * dp, axis=0, keepdims=True)
            if not first:
                shrink = jnp.exp2(m_run[:, s_cols] - top)
                total = total + l_run[:, s_cols] * shrink
                weighted = weighted + d_run[:, s_cols] * shrink
            m_run[:, s_cols] = top
            l_run[:, s_cols] = total
            d_run[:, s_cols] = weighted
            m_at[g, :, s_cols] = top
            return carry

        lax.fori_loop(0, 2, columns, 0)
        cache_t[:LATENT, rows] = cache[rows, :LATENT].T
        cache_t[LATENT:, rows] = dot_nt(eye, cache[rows, LATENT:]).astype(BF16)

    products(0)
    products(1)
    from_z(1)
    from_z(2)
    from_x(0)
    products(2)
    products(3)
    from_z(3)
    from_y(0, 1)
    from_y(0, 2)
    from_x(1)
    from_x(2)
    from_far(0)
    from_y(3, 0)
    from_y(1, 0)
    from_y(0, 3)
    from_x(3)
    from_far(1)
    from_far(2)
    for j in range(1, 4):
        from_core(0, j)
    group(0, True)
    from_far(3)
    for j in range(1, 4):
        from_y(3, j)
        from_y(1, j)
    for j in range(3):
        from_y(2, j)
    for j in range(4):
        from_core(1, j)
    group(1, False)
    from_y(2, 3)
    for j in range(4):
        from_core(3, j)
    group(3, False)
    for j in range(4):
        from_core(2, j)
    group(2, False)

    l_run[...] = 1.0 / l_run[...]
    d_run[...] = d_run[...] * l_run[...]
    d_sem = [new_sem() for _ in range(4)]

    def finish(g):
        rows = slice(g * 512, (g + 1) * 512)

        def piece(i, carry):
            part = pl.ds(pl.multiple_of(g * 512 + i * 64, 64), 64)
            weight = jnp.exp2(m_at[g] - m_run[...]) * l_run[...]
            p = e_buf[part, :] * weight
            ds_p[part, T:] = p.astype(BF16)
            ds_p[part, :T] = (p * (dp_buf[part, :] - d_run[...]) * LN2).astype(BF16)
            return carry

        lax.fori_loop(0, 8, piece, 0)
        terms = dot(ds_p[rows, :], q_rows[...])
        d_buf[g * 4:(g + 1) * 4] = terms.astype(BF16).reshape(4, ROWS, CACHE)
        send(
            d_buf.at[pl.ds(g * 4, 4), pl.ds(pl.multiple_of((1 - core) * 64, 64), 64), :],
            d_recv.at[pl.ds(g * 4, 4)], d_sem[g], partner,
        )

    def pair_sum(g):
        arrived(d_recv.at[pl.ds(g * 4, 4)], d_sem[g])

        def block(b, carry):
            own = d_buf[b, pl.ds(pl.multiple_of(core * 64, 64), 64), :]
            a_buf[b] = (own.astype(F32) + d_recv[b].astype(F32)).astype(BF16)
            return carry

        lax.fori_loop(g * 4, g * 4 + 4, block, 0)

    y_sem = [new_sem() for _ in range(6)]

    def y_rows(d):
        return pl.ds(pl.multiple_of(((y + d) % 4) * 16, 16), 16)

    lower, upper = pl.ds(0, 8), pl.ds(8, 8)
    finish(0)
    finish(1)
    pair_sum(0)
    finish(2)
    pair_sum(1)
    send(a_buf.at[lower, y_rows(2), :], y_buf.at[0], y_sem[0], y_devs[0])
    send(a_buf.at[lower, y_rows(3), :], y_buf.at[2], y_sem[2], y_devs[2])
    finish(3)
    pair_sum(2)
    pair_sum(3)
    send(a_buf.at[upper, y_rows(2), :], y_buf.at[1], y_sem[1], y_devs[2])
    send(a_buf.at[upper, y_rows(1), :], y_buf.at[3], y_sem[3], y_devs[0])

    def latent_out(c, carry):
        cols = pl.ds(pl.multiple_of(c * 256, 256), 256)
        part = dot(cache_t[...], ds_p[:, cols])
        acc[:, cols] = part
        og_t[:, cols] = part.astype(BF16)
        return carry

    lax.fori_loop(0, 4, latent_out, 0)

    for h in range(HEADS):
        cols = slice(h * 128, (h + 1) * 128)
        low = slice(T + h * 128, T + (h + 1) * 128)
        w_buf[0, :, :, cols] = (dot(og_t[:LATENT, cols], qn[:, cols]) * TO_BASE2).astype(BF16).reshape(4, 128, 128)
        w_buf[1, :, :, cols] = dot(og_t[:LATENT, low], cot[:, cols]).astype(BF16).reshape(4, 128, 128)
    wx_sem = [new_sem() for _ in range(6)]

    def at_x(d):
        return (x + d) % 4

    send(w_buf.at[0, at_x(2)], w_ring.at[0], wx_sem[0], x_devs[0])
    send(w_buf.at[1, at_x(2)], w_ring.at[1], wx_sem[1], x_devs[2])
    send(w_buf.at[0, at_x(3)], w_ring.at[2], wx_sem[2], x_devs[2])
    send(w_buf.at[1, at_x(1)], w_ring.at[3], wx_sem[3], x_devs[0])

    for h in range(HEADS):
        cols = slice(h * 128, (h + 1) * 128)
        low = slice(T + h * 128, T + (h + 1) * 128)
        out_ref[:, cols] = dot_tn(og_t[:LATENT, low], wv[:, cols]).astype(BF16)
        gqn_ref[:, cols] = (dot_tn(og_t[:LATENT, cols], wk[:, cols]) * TO_BASE2).astype(BF16)
        gqr_ref[:, h * ROPE:(h + 1) * ROPE] = (acc[LATENT:, cols].T * TO_BASE2).astype(BF16)

    stores = []

    def store(src, dst):
        copy = pltpu.make_async_copy(src, dst, out_sems.at[len(stores)])
        copy.start()
        stores.append(copy)

    store(out_ref, out_to)
    store(gqn_ref, gqn_to)
    store(gqr_ref, gqr_to)

    def y_combine(slot, base, d):
        def block(b, carry):
            own = a_buf[base + b, y_rows(d), :]
            y_out[slot, b] = (own.astype(F32) + y_buf[slot, b].astype(F32)).astype(BF16)
            return carry

        lax.fori_loop(0, 8, block, 0)

    arrived(y_buf.at[0], y_sem[0])
    y_combine(0, 0, 1)
    send(y_out.at[0], y_buf.at[4], y_sem[4], y_devs[0])
    arrived(y_buf.at[1], y_sem[1])
    y_combine(1, 8, 3)
    send(y_out.at[1], y_buf.at[5], y_sem[5], y_devs[2])

    arrived(w_ring.at[0], wx_sem[0])
    w_out[0] = (w_buf[0, at_x(1)].astype(F32) + w_ring[0].astype(F32)).astype(BF16)
    send(w_out.at[0], w_ring.at[4], wx_sem[4], x_devs[0])
    arrived(w_ring.at[1], wx_sem[1])
    w_out[1] = (w_buf[1, at_x(3)].astype(F32) + w_ring[1].astype(F32)).astype(BF16)
    send(w_out.at[1], w_ring.at[5], wx_sem[5], x_devs[2])

    for slot, sem in ((2, 2), (3, 3), (4, 4), (5, 5)):
        arrived(y_buf.at[slot], y_sem[sem])

    def y_sum(b, carry):
        first = a_buf[b, y_rows(0), :].astype(F32) + y_buf[2, b].astype(F32) + y_buf[4, b].astype(F32)
        a2_buf[b] = first.astype(BF16)
        second = a_buf[8 + b, y_rows(0), :].astype(F32) + y_buf[3, b].astype(F32) + y_buf[5, b].astype(F32)
        a2_buf[8 + b] = second.astype(BF16)
        return carry

    lax.fori_loop(0, 8, y_sum, 0)
    x_sem = [new_sem() for _ in range(3)]
    for d in range(1, 4):
        send(a2_buf.at[pl.ds(pl.multiple_of(at_x(d) * 4, 4), 4)], x_recv.at[d - 1], x_sem[d - 1], x_devs[d - 1])

    for slot, sem in ((2, 2), (3, 3), (4, 4), (5, 5)):
        arrived(w_ring.at[slot], wx_sem[sem])
    w2_buf[0] = (w_buf[0, x].astype(F32) + w_ring[2].astype(F32) + w_ring[4].astype(F32)).astype(BF16)
    w2_buf[1] = (w_buf[1, x].astype(F32) + w_ring[3].astype(F32) + w_ring[5].astype(F32)).astype(BF16)
    wz_sem = [new_sem() for _ in range(3)]

    def w_rows(d):
        return pl.ds(pl.multiple_of(((zh + d) % 4) * 32, 32), 32)

    for d in range(1, 4):
        send(w2_buf.at[:, w_rows(d), :], w_recv.at[d - 1], wz_sem[d - 1], dev(zh_to=(zh + d) % 4))

    for d in range(3):
        arrived(x_recv.at[d], x_sem[d])
    for b in range(4):
        total = a2_buf[x * 4 + b].astype(F32)
        for d in range(3):
            total = total + x_recv[d, b].astype(F32)
        a3_buf[b] = total.astype(BF16)
    zz_sem = [new_sem() for _ in range(7)]
    for d in range(7):
        send(a3_buf.at[z_peers[d] // 2], z_recv.at[d], zz_sem[d], z_devs[d])

    for d in range(3):
        arrived(w_recv.at[d], wz_sem[d])
    for kind, ref in ((0, gwk_ref), (1, gwv_ref)):
        total = w2_buf[kind, w_rows(0), :].astype(F32)
        for d in range(3):
            total = total + w_recv[d, kind].astype(F32)
        ref[...] = total
    store(gwk_ref, gwk_to)
    store(gwv_ref, gwv_to)

    for d in range(7):
        arrived(z_recv.at[d], zz_sem[d])
    total = a3_buf[zh].astype(F32)
    for d in range(7):
        total = total + z_recv[d].astype(F32)

    def gathered(dy, other):
        half = 1 - core if other else core
        return gather.at[pl.ds(pl.multiple_of(half * 64 + ((y + dy) % 4) * 16, 16), 16), :]

    mine = gathered(0, False)
    mine[...] = total.astype(BF16)
    g_sem = [[new_sem() for _ in range(4)] for _ in range(2)]
    send(mine, mine, g_sem[1][0], partner)
    for d in range(1, 4):
        send(mine, mine, g_sem[0][d], y_devs[d - 1])
        send(mine, mine, g_sem[1][d], yc_devs[d - 1])
    arrived(gathered(0, True), g_sem[1][0])
    for d in range(1, 4):
        arrived(gathered(4 - d, False), g_sem[0][d])
        arrived(gathered(4 - d, True), g_sem[1][d])
    store(gather, glat_to)
    for copy in stores:
        copy.wait()
    for copy in sent:
        copy.wait_send()
    assert counter[0] <= N_SEMS


def hand_over(lat_in, *refs):
    ins, lat_out, outs, sems = refs[:5], refs[5], refs[6:11], refs[11]
    copies = [pltpu.make_async_copy(ins[i], outs[i], sems.at[i]) for i in range(5)]
    for copy in copies:
        copy.start()
    lat_out[...] = lat_in[...].astype(F32).T
    for copy in copies:
        copy.wait()


def per_device(
    query_nope, query_rope, latent_cache, up_keys, up_values, out_grad, response_mask, boundary
):
    anywhere = pl.BlockSpec(memory_space=pl.ANY)
    vmem = pl.BlockSpec(memory_space=pltpu.VMEM)
    scratch = [
        ((CACHE, ROWS), BF16),
        ((ROWS, T), BF16), ((ROWS, HEADS * ROPE), BF16), ((LATENT, T), BF16), ((LATENT, T), BF16),
        ((ROWS, T), BF16), ((ROWS, T), BF16),
        ((SEQ, CACHE), BF16), ((CACHE, SEQ), BF16),
        ((2 * T, CACHE), BF16), ((CACHE, 2 * T), BF16),
        ((SEQ, T), F32), ((SEQ, T), F32),
        ((1, T), F32), ((1, T), F32), ((1, T), F32), ((4, 1, T), F32),
        ((SEQ, 2 * T), BF16),
        ((CACHE, 2 * T), F32), ((CACHE, 2 * T), BF16),
        ((16, ROWS, CACHE), BF16), ((16, 64, CACHE), BF16), ((16, 64, CACHE), BF16),
        ((6, 8, 16, CACHE), BF16), ((2, 8, 16, CACHE), BF16), ((16, 16, CACHE), BF16),
        ((3, 4, 16, CACHE), BF16), ((4, 16, CACHE), BF16), ((7, 16, CACHE), BF16), ((ROWS, CACHE), BF16),
        ((2, 4, 128, T), BF16), ((6, 128, T), BF16), ((2, 128, T), BF16),
        ((2, 128, T), BF16), ((3, 2, 32, T), BF16),
        ((ROWS, T), BF16), ((ROWS, T), BF16), ((ROWS, HEADS * ROPE), BF16), ((32, T), F32), ((32, T), F32),
    ]
    results = pl.pallas_call(
        kernel,
        out_shape=(
            jax.ShapeDtypeStruct((ROWS, HEADS * VDIM), BF16),
            jax.ShapeDtypeStruct((ROWS, HEADS * NOPE), BF16),
            jax.ShapeDtypeStruct((ROWS, HEADS * ROPE), BF16),
            jax.ShapeDtypeStruct((ROWS, CACHE), BF16),
            jax.ShapeDtypeStruct((32, HEADS * NOPE), F32),
            jax.ShapeDtypeStruct((32, HEADS * VDIM), F32),
        ),
        in_specs=[anywhere] * 6 + [vmem, pl.BlockSpec(memory_space=pltpu.SMEM)],
        out_specs=(anywhere,) * 6,
        scratch_shapes=[pltpu.VMEM(shape, dtype) for shape, dtype in scratch]
        + [
            pltpu.SemaphoreType.DMA((6,)),
            pltpu.SemaphoreType.DMA((6,)),
            pltpu.SemaphoreType.DMA((N_SEMS,)),
            pltpu.SemaphoreType.DMA((N_SEMS,)),
        ],
        compiler_params=pltpu.CompilerParams(
            collective_id=0, has_side_effects=True, vmem_limit_bytes=56 * 1024 * 1024
        ),
        cost_estimate=pl.CostEstimate(flops=8 * 10**9, bytes_accessed=4 * 10**6, transcendentals=10**6),
    )(
        query_nope, query_rope, latent_cache.T, up_keys, up_values, out_grad,
        response_mask.reshape(1, ROWS), boundary,
    )
    order = (3, 0, 1, 2, 4, 5)
    handed = pl.pallas_call(
        hand_over,
        out_shape=(jax.ShapeDtypeStruct((CACHE, ROWS), F32),)
        + tuple(jax.ShapeDtypeStruct(results[i].shape, results[i].dtype) for i in order[1:]),
        in_specs=[vmem] + [anywhere] * 5,
        out_specs=(vmem,) + (anywhere,) * 5,
        scratch_shapes=[pltpu.SemaphoreType.DMA((5,))],
    )(*[results[i] for i in order])
    return (handed[1], handed[2], handed[3], handed[0].T, handed[4], handed[5])


def solution(mesh):
    in_specs = (
        P("ctx", "tp"),
        P("ctx", "tp"),
        P("ctx", None),
        P(None, "tp"),
        P(None, "tp"),
        P("ctx", "tp"),
        P("ctx"),
        P(),
    )
    out_specs = (
        P("ctx", "tp"),
        P("ctx", "tp"),
        P("ctx", "tp"),
        P("ctx", None),
        P("ctx", "tp"),
        P("ctx", "tp"),
    )
    return jax.shard_map(
        per_device, mesh=mesh, in_specs=in_specs, out_specs=out_specs, check_vma=False
    )
```

```python
import math

import jax
import jax.numpy as jnp
from jax import lax
from jax.experimental import pallas as pl
from jax.experimental.pallas import tpu as pltpu
from jax.sharding import PartitionSpec as P

LATENT = 512
ROPE = 64
CACHE = LATENT + ROPE
NOPE = 128
VDIM = 128
ROWS = 128
HEADS = 4
SEQ = 2048
T = HEADS * ROWS
SCALE = 1.0 / math.sqrt(NOPE + ROPE)
LN2 = math.log(2.0)
TO_BASE2 = SCALE / LN2
MESH = pl.DeviceIdType.MESH
BF16 = jnp.bfloat16
F32 = jnp.float32
N_SEMS = 176


def dot(a, b):
    return jnp.dot(a, b, preferred_element_type=F32)


def dot_nt(a, b):
    return lax.dot_general(a, b, (((1,), (1,)), ((), ())), preferred_element_type=F32)


def dot_tn(a, b):
    return lax.dot_general(a, b, (((0,), (0,)), ((), ())), preferred_element_type=F32)


def kernel(
    qn_in, qr_in, lc_in, wk_in, wv_in, og_in, mask_ref, bound_ref,
    out_to, gqn_to, gqr_to, glat_to, gwk_to, gwv_to,
    lc, qn, qr, wk, wv, og, cot, cache, cache_t, q_rows, q_cols,
    e_buf, dp_buf, m_run, l_run, d_run, m_at, ds_p, acc, og_t,
    d_buf, d_recv, a_buf, y_recv, a2_buf, x_recv, a3_buf, z_recv, gather,
    w_buf, w_xrecv, w2_buf, w_zrecv,
    out_ref, gqn_ref, gqr_ref, gwk_ref, gwv_ref,
    in_sems, out_sems, send_sems, recv_sems,
):
    ctx, tp = lax.axis_index("ctx"), lax.axis_index("tp")
    x, zh = ctx // 4, ctx % 4
    y, zl, core = tp // 4, (tp // 2) % 2, tp % 2
    parity = y % 2

    def dev(dx=0, zh_to=None, y_to=None, zl_to=None, core_to=None):
        to_x = (x + dx) % 4
        to_zh = zh if zh_to is None else zh_to
        to_y = y if y_to is None else y_to
        to_zl = zl if zl_to is None else zl_to
        to_core = core if core_to is None else core_to
        return (to_x * 4 + to_zh, to_y * 4 + to_zl * 2 + to_core)

    counter = [0]
    sent = []

    def new_sem():
        counter[0] += 1
        return counter[0] - 1

    def send(src, dst, sem, to):
        copy = pltpu.make_async_remote_copy(
            src_ref=src, dst_ref=dst, send_sem=send_sems.at[sem], recv_sem=recv_sems.at[sem],
            device_id=to, device_id_type=MESH,
        )
        copy.start()
        sent.append(copy)

    def arrived(dst, sem):
        pltpu.make_async_remote_copy(
            src_ref=dst, dst_ref=dst, send_sem=send_sems.at[sem], recv_sem=recv_sems.at[sem],
            device_id=dev(), device_id_type=MESH,
        ).wait_recv()

    own_rows = pl.ds(pl.multiple_of(ctx * ROWS, ROWS), ROWS)
    loads = [
        pltpu.make_async_copy(src, dst, in_sems.at[i])
        for i, (src, dst) in enumerate(
            [(lc_in, lc), (qn_in, qn), (wk_in, wk), (og_in, og), (wv_in, wv), (qr_in, qr)]
        )
    ]
    for load in loads:
        load.start()
    z_at = zh * 2 + zl
    partner = dev(core_to=1 - core)
    z_peers = [((z_at + d) % 8) for d in range(1, 8)]
    z_devs = [dev(zh_to=z // 2, zl_to=z % 2) for z in z_peers]
    x_devs = [dev(dx=d) for d in range(1, 4)]
    y_devs = [dev(y_to=(y + d) % 4) for d in range(1, 4)]
    yc_devs = [dev(y_to=(y + d) % 4, core_to=1 - core) for d in range(1, 4)]
    barrier = pltpu.get_barrier_semaphore()
    peers = [partner] + z_devs + x_devs + y_devs + yc_devs
    for peer in peers:
        pl.semaphore_signal(barrier, inc=1, device_id=peer, device_id_type=MESH)
    loads[0].wait()
    whole = (
        lax.broadcasted_iota(jnp.int32, (ROWS, ROWS), 0) == lax.broadcasted_iota(jnp.int32, (ROWS, ROWS), 1)
    ).astype(F32).astype(BF16)
    cache[own_rows, :] = dot_nt(whole, lc[...]).astype(BF16)
    pl.semaphore_wait(barrier, len(peers))

    outward = zl * 2 - 1
    zh_of = [zh, (zh + outward + 4) % 4, (zh - outward + 4) % 4, (zh + 2) % 4]
    own_start = core * 64 + parity * 32
    mate_start = core * 64 + (1 - parity) * 32

    def at_x(d):
        return (x + d) % 4

    def chunk(dx, j, start, rows=32):
        block = at_x(dx) * 4 + zh_of[j]
        return cache.at[pl.ds(pl.multiple_of(block * ROWS + start, 16), rows), :]

    def sem_grid(rows, cols):
        return [[new_sem() for _ in range(cols)] for _ in range(rows)]

    z_sem = sem_grid(1, 4)[0]
    x_sem, ym_sem, yp_sem, core_sem, mate_sem = (sem_grid(4, 4) for _ in range(5))

    def same(ref, sem, to):
        send(ref, ref, sem, to)

    def along_x(j):
        for d in (2, 1, 3):
            same(chunk(0, j, own_start), x_sem[4 - d][j], x_devs[d - 1])

    def share(dx, j):
        same(chunk(dx, j, own_start, 16), ym_sem[dx][j], y_devs[0])
        same(chunk(dx, j, own_start + 16, 16), yp_sem[dx][j], y_devs[2])
        same(chunk(dx, j, own_start), core_sem[dx][j], partner)

    def from_z(j):
        arrived(chunk(0, j, own_start), z_sem[j])
        along_x(j)
        share(0, j)

    def from_x(j):
        for dx in (1, 3, 2):
            arrived(chunk(dx, j, own_start), x_sem[dx][j])
            share(dx, j)

    def from_y(dx, j):
        arrived(chunk(dx, j, mate_start, 16), ym_sem[dx][j])
        arrived(chunk(dx, j, mate_start + 16, 16), yp_sem[dx][j])
        same(chunk(dx, j, mate_start), mate_sem[dx][j], partner)

    def from_core(dx, j):
        arrived(chunk(dx, j, (1 - core) * 64 + parity * 32), core_sem[dx][j])
        arrived(chunk(dx, j, (1 - core) * 64 + (1 - parity) * 32), mate_sem[dx][j])

    same(chunk(0, 0, own_start), z_sem[3], dev(zh_to=zh_of[3], zl_to=1 - zl))
    same(chunk(0, 0, own_start), z_sem[2], dev(zh_to=zh_of[1]))
    same(chunk(0, 0, own_start), z_sem[1], dev(zh_to=zh_of[1], zl_to=1 - zl))
    along_x(0)

    for load in loads[1:]:
        load.wait()
    position = ctx * ROWS + lax.broadcasted_iota(jnp.int32, (1, ROWS), 1)
    kept = (mask_ref[...] == 1) & (position >= bound_ref[0])
    diagonal = lax.broadcasted_iota(jnp.int32, (ROWS, ROWS), 0) == lax.broadcasted_iota(
        jnp.int32, (ROWS, ROWS), 1
    )
    keep = jnp.where(diagonal & kept, 1.0, 0.0).astype(BF16)
    cot[...] = dot(keep, og[...]).astype(BF16)
    eye = (
        lax.broadcasted_iota(jnp.int32, (ROPE, ROPE), 0)
        == lax.broadcasted_iota(jnp.int32, (ROPE, ROPE), 1)
    ).astype(F32).astype(BF16)
    q_rows[T:, LATENT:] = jnp.zeros((T, ROPE), BF16)
    def products(h):
        cols = slice(h * 128, (h + 1) * 128)
        low = slice(T + h * 128, T + (h + 1) * 128)
        q_rows[cols, :LATENT] = (dot_nt(qn[:, cols], wk[:, cols]) * TO_BASE2).astype(BF16)
        q_cols[:LATENT, cols] = (dot_nt(wk[:, cols], qn[:, cols]) * TO_BASE2).astype(BF16)
        rope = (qr[:, h * ROPE:(h + 1) * ROPE].astype(F32) * TO_BASE2).astype(BF16)
        q_rows[cols, LATENT:] = rope
        q_cols[LATENT:, cols] = dot_nt(eye, rope).astype(BF16)
        q_rows[low, :LATENT] = dot_nt(cot[:, cols], wv[:, cols]).astype(BF16)
        q_cols[:LATENT, low] = dot_nt(wv[:, cols], cot[:, cols]).astype(BF16)

    def group(j, first):
        blocks = [pl.ds(pl.multiple_of((xb * 4 + zh_of[j]) * ROWS, ROWS), ROWS) for xb in range(4)]
        rows = slice(j * 512, (j + 1) * 512)

        def columns(c, carry):
            s_cols = pl.ds(pl.multiple_of(c * 256, 256), 256)
            p_cols = pl.ds(pl.multiple_of(T + c * 256, 256), 256)
            part = jnp.concatenate([cache[block, :] for block in blocks], axis=0)
            s = dot(part, q_cols[:, s_cols])
            dp = dot(part[:, :LATENT], q_cols[:LATENT, p_cols])
            dp_buf[rows, s_cols] = dp
            top = jnp.max(s, axis=0, keepdims=True)
            if not first:
                top = jnp.maximum(top, m_run[:, s_cols])
            e = jnp.exp2(s - top)
            e_buf[rows, s_cols] = e
            total = jnp.sum(e, axis=0, keepdims=True)
            weighted = jnp.sum(e * dp, axis=0, keepdims=True)
            if not first:
                shrink = jnp.exp2(m_run[:, s_cols] - top)
                total = total + l_run[:, s_cols] * shrink
                weighted = weighted + d_run[:, s_cols] * shrink
            m_run[:, s_cols] = top
            l_run[:, s_cols] = total
            d_run[:, s_cols] = weighted
            m_at[j, :, s_cols] = top
            return carry

        lax.fori_loop(0, 2, columns, 0)

    def turn(j):
        for xb in range(4):
            block = pl.ds(pl.multiple_of((xb * 4 + zh_of[j]) * ROWS, ROWS), ROWS)
            cols = slice(j * 512 + xb * ROWS, j * 512 + (xb + 1) * ROWS)
            cache_t[:LATENT, cols] = cache[block, :LATENT].T
            cache_t[LATENT:, cols] = dot_nt(eye, cache[block, LATENT:]).astype(BF16)

    for h in range(HEADS):
        products(h)
    from_z(1)
    from_z(2)
    from_z(3)
    from_x(0)
    for j in range(1, 4):
        from_y(0, j)
    from_x(1)
    from_x(2)
    for dx in range(1, 4):
        from_y(dx, 0)
    from_x(3)
    for dx in range(1, 4):
        from_core(dx, 0)
    group(0, True)
    for j in (1, 2):
        for dx in range(1, 4):
            from_y(dx, j)
    for dx in range(4):
        from_core(dx, 1)
    group(1, False)
    for dx in range(1, 4):
        from_y(dx, 3)
    for dx in range(4):
        from_core(dx, 2)
    group(2, False)
    turn(0)
    turn(1)
    turn(2)
    for dx in range(4):
        from_core(dx, 3)
    group(3, False)

    l_run[...] = 1.0 / l_run[...]
    d_run[...] = d_run[...] * l_run[...]
    d_sem = sem_grid(1, 4)[0]
    y_sem, xr_sem = sem_grid(4, 3), sem_grid(4, 3)
    zz_sem = sem_grid(4, 2)
    wx_sem, wz_sem = sem_grid(4, 3), sem_grid(4, 3)

    def finish(j):
        def piece(i, carry):
            part = pl.ds(pl.multiple_of(j * 512 + i * 64, 64), 64)
            weight = jnp.exp2(m_at[j] - m_run[...]) * l_run[...]
            p = e_buf[part, :] * weight
            ds_p[part, T:] = p.astype(BF16)
            ds_p[part, :T] = (p * (dp_buf[part, :] - d_run[...]) * LN2).astype(BF16)
            return carry

        lax.fori_loop(0, 8, piece, 0)
        terms = dot(ds_p[j * 512:(j + 1) * 512, :], q_rows[...])
        d_buf[j] = terms.astype(BF16).reshape(4, ROWS, CACHE)
        send(
            d_buf.at[j, :, pl.ds(pl.multiple_of((1 - core) * 64, 64), 64), :],
            d_recv.at[j], d_sem[j], partner,
        )

    def y_rows(d):
        return pl.ds(pl.multiple_of(((y + d) % 4) * 16, 16), 16)

    def pair_sum(j):
        arrived(d_recv.at[j], d_sem[j])

        def block(b, carry):
            own = d_buf[j, b, pl.ds(pl.multiple_of(core * 64, 64), 64), :]
            a_buf[j, b] = (own.astype(F32) + d_recv[j, b].astype(F32)).astype(BF16)
            return carry

        lax.fori_loop(0, 4, block, 0)
        for d in (2, 1, 3):
            send(a_buf.at[j, :, y_rows(d), :], y_recv.at[j, d - 1], y_sem[j][d - 1], y_devs[d - 1])

    def y_sum(j):
        for d in range(3):
            arrived(y_recv.at[j, d], y_sem[j][d])

        def block(b, carry):
            total = a_buf[j, b, y_rows(0), :].astype(F32)
            for d in range(3):
                total = total + y_recv[j, d, b].astype(F32)
            a2_buf[j, b] = total.astype(BF16)
            return carry

        lax.fori_loop(0, 4, block, 0)
        for d in (2, 1, 3):
            send(a2_buf.at[j, at_x(d)], x_recv.at[j, d - 1], xr_sem[j][d - 1], x_devs[d - 1])

    def x_sum(j):
        for d in range(3):
            arrived(x_recv.at[j, d], xr_sem[j][d])
        total = a2_buf[j, x].astype(F32)
        for d in range(3):
            total = total + x_recv[j, d].astype(F32)
        a3_buf[j] = total.astype(BF16)
        send(a3_buf.at[j], z_recv.at[j, 1], zz_sem[j][1], dev(zh_to=zh_of[j], zl_to=1 - zl))
        if j > 0:
            send(a3_buf.at[j], z_recv.at[j, 0], zz_sem[j][0], dev(zh_to=zh_of[j]))

    def latent_out(c):
        cols = slice(c * 256, (c + 1) * 256)
        part = dot(cache_t[...], ds_p[:, cols])
        acc[:, cols] = part
        og_t[:, cols] = part.astype(BF16)
        for i in range(2):
            at = slice(c * 256 + i * 128, c * 256 + (i + 1) * 128)
            heads = slice((c % 2) * 256 + i * 128, (c % 2) * 256 + (i + 1) * 128)
            rows = qn[:, heads] if c < 2 else cot[:, heads]
            terms = dot(og_t[:LATENT, at], rows) * (TO_BASE2 if c < 2 else 1.0)
            w_buf[c, :, :, i * 128:(i + 1) * 128] = terms.astype(BF16).reshape(4, 128, 128)
        for d in (2, 1, 3):
            send(w_buf.at[c, at_x(d)], w_xrecv.at[c, d - 1], wx_sem[c][d - 1], x_devs[d - 1])

    def w_rows(d):
        return pl.ds(pl.multiple_of(((zh + d) % 4) * 32, 32), 32)

    def w_x_sum(c):
        for d in range(3):
            arrived(w_xrecv.at[c, d], wx_sem[c][d])
        total = w_buf[c, x].astype(F32)
        for d in range(3):
            total = total + w_xrecv[c, d].astype(F32)
        w2_buf[c] = total.astype(BF16)
        for d in (2, 1, 3):
            send(w2_buf.at[c, w_rows(d), :], w_zrecv.at[c, d - 1], wz_sem[c][d - 1], dev(zh_to=(zh + d) % 4))

    def w_z_sum(c):
        for d in range(3):
            arrived(w_zrecv.at[c, d], wz_sem[c][d])
        total = w2_buf[c, w_rows(0), :].astype(F32)
        for d in range(3):
            total = total + w_zrecv[c, d].astype(F32)
        ref = gwk_ref if c < 2 else gwv_ref
        ref[:, (c % 2) * 256:(c % 2 + 1) * 256] = total

    def outputs(h):
        cols = slice(h * 128, (h + 1) * 128)
        low = slice(T + h * 128, T + (h + 1) * 128)
        out_ref[:, cols] = dot_tn(og_t[:LATENT, low], wv[:, cols]).astype(BF16)
        gqn_ref[:, cols] = (dot_tn(og_t[:LATENT, cols], wk[:, cols]) * TO_BASE2).astype(BF16)
        gqr_ref[:, h * ROPE:(h + 1) * ROPE] = (acc[LATENT:, cols].T * TO_BASE2).astype(BF16)

    stores = []

    def store(src, dst):
        copy = pltpu.make_async_copy(src, dst, out_sems.at[len(stores)])
        copy.start()
        stores.append(copy)

    finish(3)
    finish(1)
    pair_sum(3)
    turn(3)
    finish(2)
    pair_sum(1)
    finish(0)
    pair_sum(2)
    latent_out(0)
    pair_sum(0)
    latent_out(2)
    y_sum(3)
    latent_out(1)
    y_sum(1)
    latent_out(3)
    x_sum(3)
    w_x_sum(0)
    outputs(0)
    outputs(1)
    y_sum(2)
    x_sum(1)
    w_x_sum(2)
    outputs(2)
    outputs(3)
    store(out_ref, out_to)
    store(gqn_ref, gqn_to)
    store(gqr_ref, gqr_to)
    y_sum(0)
    w_x_sum(1)
    x_sum(2)
    w_z_sum(0)
    w_x_sum(3)
    w_z_sum(2)
    x_sum(0)
    w_z_sum(1)
    store(gwk_ref, gwk_to)
    w_z_sum(3)
    store(gwv_ref, gwv_to)

    total = a3_buf[0].astype(F32)
    for j in (3, 1, 2, 0):
        for other in range(2):
            if j > 0 or other:
                arrived(z_recv.at[j, other], zz_sem[j][other])
                total = total + z_recv[j, other].astype(F32)

    def gathered(dy, other):
        half = 1 - core if other else core
        return gather.at[pl.ds(pl.multiple_of(half * 64 + ((y + dy) % 4) * 16, 16), 16), :]

    mine = gathered(0, False)
    mine[...] = total.astype(BF16)
    g_sem = sem_grid(2, 4)
    for d in (2, 1, 3):
        same(mine, g_sem[0][d], y_devs[d - 1])
        same(mine, g_sem[1][d], yc_devs[d - 1])
    same(mine, g_sem[1][0], partner)
    arrived(gathered(0, True), g_sem[1][0])
    for d in range(1, 4):
        arrived(gathered(4 - d, False), g_sem[0][d])
        arrived(gathered(4 - d, True), g_sem[1][d])
    store(gather, glat_to)
    for copy in stores:
        copy.wait()
    for copy in sent:
        copy.wait_send()
    assert counter[0] <= N_SEMS


def hand_over(lat_in, *refs):
    ins, lat_out, outs = refs[:5], refs[5], refs[6:11]
    for source, target in zip(ins, outs):
        target[...] = source[...]
    lat_out[...] = lat_in[...].astype(F32).T


def per_device(
    query_nope, query_rope, latent_cache, up_keys, up_values, out_grad, response_mask, boundary
):
    anywhere = pl.BlockSpec(memory_space=pl.ANY)
    vmem = pl.BlockSpec(memory_space=pltpu.VMEM)
    scratch = [
        ((CACHE, ROWS), BF16),
        ((ROWS, T), BF16), ((ROWS, HEADS * ROPE), BF16), ((LATENT, T), BF16), ((LATENT, T), BF16),
        ((ROWS, T), BF16), ((ROWS, T), BF16),
        ((SEQ, CACHE), BF16), ((CACHE, SEQ), BF16),
        ((2 * T, CACHE), BF16), ((CACHE, 2 * T), BF16),
        ((SEQ, T), F32), ((SEQ, T), F32),
        ((1, T), F32), ((1, T), F32), ((1, T), F32), ((4, 1, T), F32),
        ((SEQ, 2 * T), BF16),
        ((CACHE, 2 * T), F32), ((CACHE, 2 * T), BF16),
        ((4, 4, ROWS, CACHE), BF16), ((4, 4, 64, CACHE), BF16), ((4, 4, 64, CACHE), BF16),
        ((4, 3, 4, 16, CACHE), BF16), ((4, 4, 16, CACHE), BF16), ((4, 3, 16, CACHE), BF16),
        ((4, 16, CACHE), BF16), ((4, 2, 16, CACHE), BF16), ((ROWS, CACHE), BF16),
        ((4, 4, 128, 256), BF16), ((4, 3, 128, 256), BF16), ((4, 128, 256), BF16), ((4, 3, 32, 256), BF16),
        ((ROWS, T), BF16), ((ROWS, T), BF16), ((ROWS, HEADS * ROPE), BF16), ((32, T), F32), ((32, T), F32),
    ]
    results = pl.pallas_call(
        kernel,
        out_shape=(
            jax.ShapeDtypeStruct((ROWS, HEADS * VDIM), BF16),
            jax.ShapeDtypeStruct((ROWS, HEADS * NOPE), BF16),
            jax.ShapeDtypeStruct((ROWS, HEADS * ROPE), BF16),
            jax.ShapeDtypeStruct((ROWS, CACHE), BF16),
            jax.ShapeDtypeStruct((32, HEADS * NOPE), F32),
            jax.ShapeDtypeStruct((32, HEADS * VDIM), F32),
        ),
        in_specs=[anywhere] * 6 + [vmem, pl.BlockSpec(memory_space=pltpu.SMEM)],
        out_specs=(anywhere,) * 6,
        scratch_shapes=[pltpu.VMEM(shape, dtype) for shape, dtype in scratch]
        + [
            pltpu.SemaphoreType.DMA((6,)),
            pltpu.SemaphoreType.DMA((6,)),
            pltpu.SemaphoreType.DMA((N_SEMS,)),
            pltpu.SemaphoreType.DMA((N_SEMS,)),
        ],
        compiler_params=pltpu.CompilerParams(
            collective_id=0, has_side_effects=True, vmem_limit_bytes=56 * 1024 * 1024
        ),
        cost_estimate=pl.CostEstimate(flops=8 * 10**9, bytes_accessed=4 * 10**6, transcendentals=10**6),
    )(
        query_nope, query_rope, latent_cache.T, up_keys, up_values, out_grad,
        response_mask.reshape(1, ROWS), boundary,
    )
    order = (3, 0, 1, 2, 4, 5)
    handed = pl.pallas_call(
        hand_over,
        out_shape=(jax.ShapeDtypeStruct((CACHE, ROWS), F32),)
        + tuple(jax.ShapeDtypeStruct(results[i].shape, results[i].dtype) for i in order[1:]),
        in_specs=[vmem] * 6,
        out_specs=(vmem,) * 6,
    )(*[results[i] for i in order])
    return (handed[1], handed[2], handed[3], handed[0].T, handed[4], handed[5])


def solution(mesh):
    in_specs = (
        P("ctx", "tp"),
        P("ctx", "tp"),
        P("ctx", None),
        P(None, "tp"),
        P(None, "tp"),
        P("ctx", "tp"),
        P("ctx"),
        P(),
    )
    out_specs = (
        P("ctx", "tp"),
        P("ctx", "tp"),
        P("ctx", "tp"),
        P("ctx", None),
        P("ctx", "tp"),
        P("ctx", "tp"),
    )
    return jax.shard_map(
        per_device, mesh=mesh, in_specs=in_specs, out_specs=out_specs, check_vma=False
    )
```

```python
import math

import jax
import jax.numpy as jnp
from jax import lax
from jax.experimental import pallas as pl
from jax.experimental.pallas import tpu as pltpu
from jax.sharding import PartitionSpec as P

LATENT = 512
ROPE = 64
CACHE = LATENT + ROPE
NOPE = 128
VDIM = 128
ROWS = 128
HEADS = 4
SEQ = 2048
T = HEADS * ROWS
SCALE = 1.0 / math.sqrt(NOPE + ROPE)
LN2 = math.log(2.0)
TO_BASE2 = SCALE / LN2
MAIN = 384
SIDE = CACHE - MAIN
MESH = pl.DeviceIdType.MESH
BF16 = jnp.bfloat16
F32 = jnp.float32
N_SEMS = 208


def dot(a, b):
    return jnp.dot(a, b, preferred_element_type=F32)


def dot_nt(a, b):
    return lax.dot_general(a, b, (((1,), (1,)), ((), ())), preferred_element_type=F32)


def dot_tn(a, b):
    return lax.dot_general(a, b, (((0,), (0,)), ((), ())), preferred_element_type=F32)


def kernel(
    qn_in, qr_in, lc_in, wk_in, wv_in, og_in, mask_ref, bound_ref,
    out_to, gqn_to, gqr_to, glat_to, gwk_to, gwv_to,
    lc, qn, qr, wk, wv, og, cot, cache, cache_t, q_rows, q_cols,
    e_buf, dp_buf, m_run, l_run, d_run, m_at, ds_p, acc, og_t,
    s_buf, side_recv, sx_buf, sx_recv, sy_buf, sy_recv,
    d_buf, d_recv, a_buf, y_recv, a2_buf, x_recv, a3_buf, z_recv, gather,
    w_buf, w_xrecv, w2_buf, w_zrecv,
    out_ref, gqn_ref, gqr_ref, gwk_ref, gwv_ref,
    in_sems, out_sems, send_sems, recv_sems,
):
    ctx, tp = lax.axis_index("ctx"), lax.axis_index("tp")
    x, zh = ctx // 4, ctx % 4
    y, zl, core = tp // 4, (tp // 2) % 2, tp % 2
    parity = y % 2

    def dev(dx=0, zh_to=None, y_to=None, zl_to=None, core_to=None):
        to_x = (x + dx) % 4
        to_zh = zh if zh_to is None else zh_to
        to_y = y if y_to is None else y_to
        to_zl = zl if zl_to is None else zl_to
        to_core = core if core_to is None else core_to
        return (to_x * 4 + to_zh, to_y * 4 + to_zl * 2 + to_core)

    counter = [0]
    sent = []

    def new_sem():
        counter[0] += 1
        return counter[0] - 1

    def send(src, dst, sem, to):
        copy = pltpu.make_async_remote_copy(
            src_ref=src, dst_ref=dst, send_sem=send_sems.at[sem], recv_sem=recv_sems.at[sem],
            device_id=to, device_id_type=MESH,
        )
        copy.start()
        sent.append(copy)

    def arrived(dst, sem):
        pltpu.make_async_remote_copy(
            src_ref=dst, dst_ref=dst, send_sem=send_sems.at[sem], recv_sem=recv_sems.at[sem],
            device_id=dev(), device_id_type=MESH,
        ).wait_recv()

    own_rows = pl.ds(pl.multiple_of(ctx * ROWS, ROWS), ROWS)
    loads = [
        pltpu.make_async_copy(src, dst, in_sems.at[i])
        for i, (src, dst) in enumerate(
            [(lc_in, lc), (qn_in, qn), (wk_in, wk), (og_in, og), (wv_in, wv), (qr_in, qr)]
        )
    ]
    for load in loads:
        load.start()
    z_at = zh * 2 + zl
    partner = dev(core_to=1 - core)
    z_peers = [((z_at + d) % 8) for d in range(1, 8)]
    z_devs = [dev(zh_to=z // 2, zl_to=z % 2) for z in z_peers]
    x_devs = [dev(dx=d) for d in range(1, 4)]
    y_devs = [dev(y_to=(y + d) % 4) for d in range(1, 4)]
    yc_devs = [dev(y_to=(y + d) % 4, core_to=1 - core) for d in range(1, 4)]
    barrier = pltpu.get_barrier_semaphore()
    twin = dev(zl_to=1 - zl)
    twin_other = dev(zl_to=1 - zl, core_to=1 - core)
    peers = [partner, twin_other] + z_devs + x_devs + y_devs + yc_devs
    for peer in peers:
        pl.semaphore_signal(barrier, inc=1, device_id=peer, device_id_type=MESH)
    loads[0].wait()
    whole = (
        lax.broadcasted_iota(jnp.int32, (ROWS, ROWS), 0) == lax.broadcasted_iota(jnp.int32, (ROWS, ROWS), 1)
    ).astype(F32).astype(BF16)
    cache[own_rows, :] = dot_nt(whole, lc[...]).astype(BF16)
    pl.semaphore_wait(barrier, len(peers))

    outward = zl * 2 - 1
    zh_of = [zh, (zh + outward + 4) % 4, (zh - outward + 4) % 4, (zh + 2) % 4]
    own_start = core * 64 + parity * 32
    mate_start = core * 64 + (1 - parity) * 32

    def at_x(d):
        return (x + d) % 4

    def chunk(dx, j, start, rows=32):
        block = at_x(dx) * 4 + zh_of[j]
        return cache.at[pl.ds(pl.multiple_of(block * ROWS + start, 16), rows), :]

    def sem_grid(rows, cols):
        return [[new_sem() for _ in range(cols)] for _ in range(rows)]

    z_sem = sem_grid(1, 4)[0]
    x_sem, ym_sem, yp_sem, core_sem, mate_sem = (sem_grid(4, 4) for _ in range(5))

    def same(ref, sem, to):
        send(ref, ref, sem, to)

    def along_x(j):
        for d in (2, 1, 3):
            same(chunk(0, j, own_start), x_sem[4 - d][j], x_devs[d - 1])

    def share(dx, j):
        same(chunk(dx, j, own_start, 16), ym_sem[dx][j], y_devs[0])
        same(chunk(dx, j, own_start + 16, 16), yp_sem[dx][j], y_devs[2])
        same(chunk(dx, j, own_start), core_sem[dx][j], partner)

    def from_z(j):
        arrived(chunk(0, j, own_start), z_sem[j])
        along_x(j)
        share(0, j)

    def from_x(j):
        for dx in (1, 3, 2):
            arrived(chunk(dx, j, own_start), x_sem[dx][j])
            share(dx, j)

    def from_y(dx, j):
        arrived(chunk(dx, j, mate_start, 16), ym_sem[dx][j])
        arrived(chunk(dx, j, mate_start + 16, 16), yp_sem[dx][j])
        same(chunk(dx, j, mate_start), mate_sem[dx][j], partner)

    def from_core(dx, j):
        arrived(chunk(dx, j, (1 - core) * 64 + parity * 32), core_sem[dx][j])
        arrived(chunk(dx, j, (1 - core) * 64 + (1 - parity) * 32), mate_sem[dx][j])

    same(chunk(0, 0, own_start), z_sem[1], dev(zh_to=zh_of[1], zl_to=1 - zl))
    same(chunk(0, 0, own_start), z_sem[2], dev(zh_to=zh_of[1]))
    same(chunk(0, 0, own_start), z_sem[3], dev(zh_to=zh_of[3], zl_to=1 - zl))
    along_x(0)

    for load in loads[1:]:
        load.wait()
    position = ctx * ROWS + lax.broadcasted_iota(jnp.int32, (1, ROWS), 1)
    kept = (mask_ref[...] == 1) & (position >= bound_ref[0])
    diagonal = lax.broadcasted_iota(jnp.int32, (ROWS, ROWS), 0) == lax.broadcasted_iota(
        jnp.int32, (ROWS, ROWS), 1
    )
    keep = jnp.where(diagonal & kept, 1.0, 0.0).astype(BF16)
    cot[...] = dot(keep, og[...]).astype(BF16)
    eye = (
        lax.broadcasted_iota(jnp.int32, (ROPE, ROPE), 0)
        == lax.broadcasted_iota(jnp.int32, (ROPE, ROPE), 1)
    ).astype(F32).astype(BF16)
    q_rows[T:, LATENT:] = jnp.zeros((T, ROPE), BF16)
    def products(h):
        cols = slice(h * 128, (h + 1) * 128)
        low = slice(T + h * 128, T + (h + 1) * 128)
        q_rows[cols, :LATENT] = (dot_nt(qn[:, cols], wk[:, cols]) * TO_BASE2).astype(BF16)
        q_cols[:LATENT, cols] = (dot_nt(wk[:, cols], qn[:, cols]) * TO_BASE2).astype(BF16)
        rope = (qr[:, h * ROPE:(h + 1) * ROPE].astype(F32) * TO_BASE2).astype(BF16)
        q_rows[cols, LATENT:] = rope
        q_cols[LATENT:, cols] = dot_nt(eye, rope).astype(BF16)
        q_rows[low, :LATENT] = dot_nt(cot[:, cols], wv[:, cols]).astype(BF16)
        q_cols[:LATENT, low] = dot_nt(wv[:, cols], cot[:, cols]).astype(BF16)

    def group(j, first):
        blocks = [pl.ds(pl.multiple_of((xb * 4 + zh_of[j]) * ROWS, ROWS), ROWS) for xb in range(4)]
        rows = slice(j * 512, (j + 1) * 512)

        for c in range(2):
            s_cols = slice(c * 256, (c + 1) * 256)
            p_cols = slice(T + c * 256, T + (c + 1) * 256)
            part = jnp.concatenate([cache[block, :] for block in blocks], axis=0)
            s = dot(part, q_cols[:, s_cols])
            dp = dot(part[:, :LATENT], q_cols[:LATENT, p_cols])
            dp_buf[rows, s_cols] = dp
            top = jnp.max(s, axis=0, keepdims=True)
            if not first:
                top = jnp.maximum(top, m_run[:, s_cols])
            e = jnp.exp2(s - top)
            e_buf[rows, s_cols] = e
            total = jnp.sum(e, axis=0, keepdims=True)
            weighted = jnp.sum(e * dp, axis=0, keepdims=True)
            if not first:
                shrink = jnp.exp2(m_run[:, s_cols] - top)
                total = total + l_run[:, s_cols] * shrink
                weighted = weighted + d_run[:, s_cols] * shrink
            m_run[:, s_cols] = top
            l_run[:, s_cols] = total
            d_run[:, s_cols] = weighted
            m_at[j, :, s_cols] = top

    def turn(j):
        for xb in range(4):
            block = pl.ds(pl.multiple_of((xb * 4 + zh_of[j]) * ROWS, ROWS), ROWS)
            cols = slice(j * 512 + xb * ROWS, j * 512 + (xb + 1) * ROWS)
            cache_t[:LATENT, cols] = cache[block, :LATENT].T
            cache_t[LATENT:, cols] = dot_nt(eye, cache[block, LATENT:]).astype(BF16)

    products(0)
    products(1)
    from_z(1)
    products(2)
    from_z(2)
    products(3)
    from_x(0)
    from_z(3)
    from_x(1)
    for j in range(1, 4):
        from_y(0, j)
    for dx in range(1, 4):
        from_y(dx, 0)
    for dx in range(1, 4):
        from_core(dx, 0)
    group(0, True)
    from_x(2)
    for dx in range(1, 4):
        from_y(dx, 1)
    from_x(3)
    for dx in range(4):
        from_core(dx, 1)
    group(1, False)
    for j in (2, 3):
        for dx in range(1, 4):
            from_y(dx, j)
    for dx in range(4):
        from_core(dx, 2)
    group(2, False)
    for j in range(3):
        turn(j)
    for dx in range(4):
        from_core(dx, 3)
    group(3, False)

    l_run[...] = 1.0 / l_run[...]
    d_run[...] = d_run[...] * l_run[...]
    d_sem = sem_grid(1, 4)[0]
    y_sem, xr_sem = sem_grid(4, 3), sem_grid(4, 3)
    zz_sem, side_z_sem = sem_grid(4, 2), sem_grid(4, 2)
    side_x_sem, side_y_sem = sem_grid(1, 3)[0], sem_grid(1, 3)[0]
    wx_sem, wz_sem = sem_grid(4, 3), sem_grid(4, 3)

    def probabilities(j):
        weight = jnp.exp2(m_at[j] - m_run[...]) * l_run[...]
        delta = d_run[...]
        for i in range(16):
            part = slice(j * 512 + i * 32, j * 512 + (i + 1) * 32)
            p = e_buf[part, :] * weight
            ds_p[part, T:] = p.astype(BF16)
            ds_p[part, :T] = (p * (dp_buf[part, :] - delta) * LN2).astype(BF16)

    def cache_terms(j):
        terms = dot(ds_p[j * 512:(j + 1) * 512, :], q_rows[...])
        d_buf[j] = terms.astype(BF16).reshape(4, ROWS, CACHE)
        send(
            d_buf.at[j, :, pl.ds(pl.multiple_of((1 - core) * 64, 64), 64), :],
            d_recv.at[j], d_sem[j], partner,
        )

    def y_rows(d):
        return pl.ds(pl.multiple_of(((y + d) % 4) * 16, 16), 16)

    def l_rows(l):
        return pl.ds(pl.multiple_of(l * 32, 32), 32)

    def pair_sum(j):
        arrived(d_recv.at[j], d_sem[j])

        def block(b, carry):
            own = d_buf[j, b, pl.ds(pl.multiple_of(core * 64, 64), 64), :]
            total = (own.astype(F32) + d_recv[j, b].astype(F32)).astype(BF16)
            a_buf[j, b] = total[:, :MAIN]
            s_buf[j, b] = total[:, MAIN:]
            return carry

        lax.fori_loop(0, 4, block, 0)
        for d in (2, 1, 3):
            send(a_buf.at[j, :, y_rows(d), :], y_recv.at[j, d - 1], y_sem[j][d - 1], y_devs[d - 1])
        send(s_buf.at[j, :, l_rows(1 - zl), :], side_recv.at[j, 1], side_z_sem[j][1], dev(zh_to=zh_of[j], zl_to=1 - zl))
        if j > 0:
            send(s_buf.at[j, :, l_rows(zl), :], side_recv.at[j, 0], side_z_sem[j][0], dev(zh_to=zh_of[j]))

    def y_sum(j):
        for d in range(3):
            arrived(y_recv.at[j, d], y_sem[j][d])

        def block(b, carry):
            total = a_buf[j, b, y_rows(0), :].astype(F32)
            for d in range(3):
                total = total + y_recv[j, d, b].astype(F32)
            a2_buf[j, b] = total.astype(BF16)
            return carry

        lax.fori_loop(0, 4, block, 0)
        for d in (2, 1, 3):
            send(a2_buf.at[j, at_x(d)], x_recv.at[j, d - 1], xr_sem[j][d - 1], x_devs[d - 1])

    def x_sum(j):
        for d in range(3):
            arrived(x_recv.at[j, d], xr_sem[j][d])
        total = a2_buf[j, x].astype(F32)
        for d in range(3):
            total = total + x_recv[j, d].astype(F32)
        a3_buf[j] = total.astype(BF16)
        send(a3_buf.at[j], z_recv.at[j, 1], zz_sem[j][1], dev(zh_to=zh_of[j], zl_to=1 - zl))
        if j > 0:
            send(a3_buf.at[j], z_recv.at[j, 0], zz_sem[j][0], dev(zh_to=zh_of[j]))

    def side_z_sum():
        slots = [(j, other) for j in (3, 1, 2, 0) for other in range(2) if j > 0 or other]
        for j, other in slots:
            arrived(side_recv.at[j, other], side_z_sem[j][other])

        def block(b, carry):
            total = s_buf[0, b, l_rows(zl), :].astype(F32)
            for j, other in slots:
                total = total + side_recv[j, other, b].astype(F32)
            sx_buf[b] = total.astype(BF16)
            return carry

        lax.fori_loop(0, 4, block, 0)
        for d in (2, 1, 3):
            send(sx_buf.at[at_x(d)], sx_recv.at[d - 1], side_x_sem[d - 1], x_devs[d - 1])

    def side_x_sum():
        for d in range(3):
            arrived(sx_recv.at[d], side_x_sem[d])
        total = sx_buf[x].astype(F32)
        for d in range(3):
            total = total + sx_recv[d].astype(F32)
        sy_buf[...] = total.astype(BF16)
        for d in (2, 1, 3):
            send(sy_buf, sy_recv.at[d - 1], side_y_sem[d - 1], y_devs[d - 1])

    def latent_out(c):
        cols = slice(c * 256, (c + 1) * 256)
        part = dot(cache_t[...], ds_p[:, cols])
        acc[:, cols] = part
        og_t[:, cols] = part.astype(BF16)
        for i in range(2):
            at = slice(c * 256 + i * 128, c * 256 + (i + 1) * 128)
            heads = slice((c % 2) * 256 + i * 128, (c % 2) * 256 + (i + 1) * 128)
            rows = qn[:, heads] if c < 2 else cot[:, heads]
            terms = dot(og_t[:LATENT, at], rows) * (TO_BASE2 if c < 2 else 1.0)
            w_buf[c, :, :, i * 128:(i + 1) * 128] = terms.astype(BF16).reshape(4, 128, 128)
        for d in (2, 1, 3):
            send(w_buf.at[c, at_x(d)], w_xrecv.at[c, d - 1], wx_sem[c][d - 1], x_devs[d - 1])

    def w_rows(d):
        return pl.ds(pl.multiple_of(((zh + d) % 4) * 32, 32), 32)

    def w_x_sum(c):
        for d in range(3):
            arrived(w_xrecv.at[c, d], wx_sem[c][d])
        total = w_buf[c, x].astype(F32)
        for d in range(3):
            total = total + w_xrecv[c, d].astype(F32)
        w2_buf[c] = total.astype(BF16)
        for d in (2, 1, 3):
            send(w2_buf.at[c, w_rows(d), :], w_zrecv.at[c, d - 1], wz_sem[c][d - 1], dev(zh_to=(zh + d) % 4))

    def w_z_sum(c):
        for d in range(3):
            arrived(w_zrecv.at[c, d], wz_sem[c][d])
        total = w2_buf[c, w_rows(0), :].astype(F32)
        for d in range(3):
            total = total + w_zrecv[c, d].astype(F32)
        ref = gwk_ref if c < 2 else gwv_ref
        ref[:, (c % 2) * 256:(c % 2 + 1) * 256] = total

    def outputs(h):
        cols = slice(h * 128, (h + 1) * 128)
        low = slice(T + h * 128, T + (h + 1) * 128)
        out_ref[:, cols] = dot_tn(og_t[:LATENT, low], wv[:, cols]).astype(BF16)
        gqn_ref[:, cols] = (dot_tn(og_t[:LATENT, cols], wk[:, cols]) * TO_BASE2).astype(BF16)
        gqr_ref[:, h * ROPE:(h + 1) * ROPE] = (acc[LATENT:, cols].T * TO_BASE2).astype(BF16)

    stores = []

    def store(src, dst):
        copy = pltpu.make_async_copy(src, dst, out_sems.at[len(stores)])
        copy.start()
        stores.append(copy)

    probabilities(3)
    probabilities(1)
    cache_terms(3)
    probabilities(2)
    cache_terms(1)
    pair_sum(3)
    probabilities(0)
    cache_terms(2)
    pair_sum(1)
    turn(3)
    cache_terms(0)
    latent_out(0)
    pair_sum(2)
    latent_out(2)
    pair_sum(0)
    y_sum(3)
    latent_out(1)
    y_sum(1)
    latent_out(3)
    y_sum(2)
    for h in range(HEADS):
        outputs(h)
    store(out_ref, out_to)
    store(gqn_ref, gqn_to)
    store(gqr_ref, gqr_to)
    w_x_sum(0)
    y_sum(0)
    side_z_sum()
    x_sum(3)
    x_sum(1)
    w_x_sum(2)
    x_sum(2)
    w_x_sum(1)
    x_sum(0)
    side_x_sum()

    total = a3_buf[0].astype(F32)
    for j in (3, 1, 2, 0):
        for other in range(2):
            if j > 0 or other:
                arrived(z_recv.at[j, other], zz_sem[j][other])
                total = total + z_recv[j, other].astype(F32)

    def gathered(dy, other):
        half = 1 - core if other else core
        return gather.at[pl.ds(pl.multiple_of(half * 64 + ((y + dy) % 4) * 16, 16), 16), pl.ds(0, MAIN)]

    mine = gathered(0, False)
    mine[...] = total.astype(BF16)
    g_sem = sem_grid(2, 4)
    for d in (2, 1, 3):
        same(mine, g_sem[0][d], y_devs[d - 1])
        same(mine, g_sem[1][d], yc_devs[d - 1])
    same(mine, g_sem[1][0], partner)

    for d in range(3):
        arrived(sy_recv.at[d], side_y_sem[d])
    total = sy_buf[...].astype(F32)
    for d in range(3):
        total = total + sy_recv[d].astype(F32)

    def side_gathered(other_l, other_core):
        l = 1 - zl if other_l else zl
        half = 1 - core if other_core else core
        return gather.at[pl.ds(pl.multiple_of(half * 64 + l * 32, 32), 32), pl.ds(MAIN, SIDE)]

    side = side_gathered(False, False)
    side[...] = total.astype(BF16)
    side_sem = sem_grid(2, 2)
    same(side, side_sem[1][0], twin)
    same(side, side_sem[1][1], twin_other)
    same(side, side_sem[0][1], partner)
    w_x_sum(3)
    for c in (0, 2, 1, 3):
        w_z_sum(c)
    store(gwk_ref, gwk_to)
    store(gwv_ref, gwv_to)
    arrived(gathered(0, True), g_sem[1][0])
    for d in range(1, 4):
        arrived(gathered(4 - d, False), g_sem[0][d])
        arrived(gathered(4 - d, True), g_sem[1][d])
    for other_l, other_core in ((1, 0), (1, 1), (0, 1)):
        arrived(side_gathered(other_l, other_core), side_sem[other_l][other_core])
    store(gather, glat_to)
    for copy in stores:
        copy.wait()
    for copy in sent:
        copy.wait_send()
    assert counter[0] <= N_SEMS


def hand_over(lat_in, *refs):
    ins, lat_out, outs = refs[:5], refs[5], refs[6:11]
    for source, target in zip(ins, outs):
        target[...] = source[...]
    lat_out[...] = lat_in[...].astype(F32).T


def per_device(
    query_nope, query_rope, latent_cache, up_keys, up_values, out_grad, response_mask, boundary
):
    anywhere = pl.BlockSpec(memory_space=pl.ANY)
    vmem = pl.BlockSpec(memory_space=pltpu.VMEM)
    scratch = [
        ((CACHE, ROWS), BF16),
        ((ROWS, T), BF16), ((ROWS, HEADS * ROPE), BF16), ((LATENT, T), BF16), ((LATENT, T), BF16),
        ((ROWS, T), BF16), ((ROWS, T), BF16),
        ((SEQ, CACHE), BF16), ((CACHE, SEQ), BF16),
        ((2 * T, CACHE), BF16), ((CACHE, 2 * T), BF16),
        ((SEQ, T), F32), ((SEQ, T), F32),
        ((1, T), F32), ((1, T), F32), ((1, T), F32), ((4, 1, T), F32),
        ((SEQ, 2 * T), BF16),
        ((CACHE, 2 * T), F32), ((CACHE, 2 * T), BF16),
        ((4, 4, 64, SIDE), BF16), ((4, 2, 4, 32, SIDE), BF16), ((4, 32, SIDE), BF16),
        ((3, 32, SIDE), BF16), ((32, SIDE), BF16), ((3, 32, SIDE), BF16),
        ((4, 4, ROWS, CACHE), BF16), ((4, 4, 64, CACHE), BF16), ((4, 4, 64, MAIN), BF16),
        ((4, 3, 4, 16, MAIN), BF16), ((4, 4, 16, MAIN), BF16), ((4, 3, 16, MAIN), BF16),
        ((4, 16, MAIN), BF16), ((4, 2, 16, MAIN), BF16), ((ROWS, CACHE), BF16),
        ((4, 4, 128, 256), BF16), ((4, 3, 128, 256), BF16), ((4, 128, 256), BF16), ((4, 3, 32, 256), BF16),
        ((ROWS, T), BF16), ((ROWS, T), BF16), ((ROWS, HEADS * ROPE), BF16), ((32, T), F32), ((32, T), F32),
    ]
    results = pl.pallas_call(
        kernel,
        out_shape=(
            jax.ShapeDtypeStruct((ROWS, HEADS * VDIM), BF16),
            jax.ShapeDtypeStruct((ROWS, HEADS * NOPE), BF16),
            jax.ShapeDtypeStruct((ROWS, HEADS * ROPE), BF16),
            jax.ShapeDtypeStruct((ROWS, CACHE), BF16),
            jax.ShapeDtypeStruct((32, HEADS * NOPE), F32),
            jax.ShapeDtypeStruct((32, HEADS * VDIM), F32),
        ),
        in_specs=[anywhere] * 6 + [vmem, pl.BlockSpec(memory_space=pltpu.SMEM)],
        out_specs=(anywhere,) * 6,
        scratch_shapes=[pltpu.VMEM(shape, dtype) for shape, dtype in scratch]
        + [
            pltpu.SemaphoreType.DMA((6,)),
            pltpu.SemaphoreType.DMA((6,)),
            pltpu.SemaphoreType.DMA((N_SEMS,)),
            pltpu.SemaphoreType.DMA((N_SEMS,)),
        ],
        compiler_params=pltpu.CompilerParams(
            collective_id=0, has_side_effects=True, vmem_limit_bytes=56 * 1024 * 1024
        ),
        cost_estimate=pl.CostEstimate(flops=8 * 10**9, bytes_accessed=4 * 10**6, transcendentals=10**6),
    )(
        query_nope, query_rope, latent_cache.T, up_keys, up_values, out_grad,
        response_mask.reshape(1, ROWS), boundary,
    )
    order = (3, 0, 1, 2, 4, 5)
    handed = pl.pallas_call(
        hand_over,
        out_shape=(jax.ShapeDtypeStruct((CACHE, ROWS), F32),)
        + tuple(jax.ShapeDtypeStruct(results[i].shape, results[i].dtype) for i in order[1:]),
        in_specs=[vmem] * 6,
        out_specs=(vmem,) * 6,
    )(*[results[i] for i in order])
    return (handed[1], handed[2], handed[3], handed[0].T, handed[4], handed[5])


def solution(mesh):
    in_specs = (
        P("ctx", "tp"),
        P("ctx", "tp"),
        P("ctx", None),
        P(None, "tp"),
        P(None, "tp"),
        P("ctx", "tp"),
        P("ctx"),
        P(),
    )
    out_specs = (
        P("ctx", "tp"),
        P("ctx", "tp"),
        P("ctx", "tp"),
        P("ctx", None),
        P("ctx", "tp"),
        P("ctx", "tp"),
    )
    return jax.shard_map(
        per_device, mesh=mesh, in_specs=in_specs, out_specs=out_specs, check_vma=False
    )
```

```python
import math

import jax
import jax.numpy as jnp
from jax import lax
from jax.experimental import pallas as pl
from jax.experimental.pallas import tpu as pltpu
from jax.sharding import PartitionSpec as P

LATENT = 512
ROPE = 64
CACHE = LATENT + ROPE
NOPE = 128
VDIM = 128
ROWS = 128
HEADS = 4
SEQ = 2048
T = HEADS * ROWS
SCALE = 1.0 / math.sqrt(NOPE + ROPE)
LN2 = math.log(2.0)
TO_BASE2 = SCALE / LN2
MAIN = 384
SIDE = CACHE - MAIN
MESH = pl.DeviceIdType.MESH
BF16 = jnp.bfloat16
F32 = jnp.float32
N_SEMS = 208


def dot(a, b):
    return jnp.dot(a, b, preferred_element_type=F32)


def dot_nt(a, b):
    return lax.dot_general(a, b, (((1,), (1,)), ((), ())), preferred_element_type=F32)


def dot_tn(a, b):
    return lax.dot_general(a, b, (((0,), (0,)), ((), ())), preferred_element_type=F32)


def kernel(
    qn_in, qr_in, lc_in, wk_in, wv_in, og_in, mask_ref, bound_ref,
    out_to, gqn_to, gqr_to, glat_to, gwk_to, gwv_to,
    lc, qn, qr, wk, wv, og, cot, cache, cache_t, q_rows, q_cols,
    e_buf, dp_buf, m_run, l_run, d_run, m_at, ds_p, acc, og_t,
    s_buf, side_recv, sx_buf, sx_recv, g_main, g_side,
    d_buf, d_recv, a_buf, y_recv, a2_buf, x_recv, a3_buf, z_recv, gather,
    w_buf, w_xrecv, w2_buf, w_zrecv,
    out_ref, gqn_ref, gqr_ref, gwk_ref, gwv_ref,
    in_sems, out_sems, send_sems, recv_sems,
):
    ctx, tp = lax.axis_index("ctx"), lax.axis_index("tp")
    x, zh = ctx // 4, ctx % 4
    y, zl, core = tp // 4, (tp // 2) % 2, tp % 2
    parity = y % 2

    def dev(dx=0, zh_to=None, y_to=None, zl_to=None, core_to=None):
        to_x = (x + dx) % 4
        to_zh = zh if zh_to is None else zh_to
        to_y = y if y_to is None else y_to
        to_zl = zl if zl_to is None else zl_to
        to_core = core if core_to is None else core_to
        return (to_x * 4 + to_zh, to_y * 4 + to_zl * 2 + to_core)

    counter = [0]
    sent = []

    def new_sem():
        counter[0] += 1
        return counter[0] - 1

    def send(src, dst, sem, to):
        copy = pltpu.make_async_remote_copy(
            src_ref=src, dst_ref=dst, send_sem=send_sems.at[sem], recv_sem=recv_sems.at[sem],
            device_id=to, device_id_type=MESH,
        )
        copy.start()
        sent.append(copy)

    def arrived(dst, sem):
        pltpu.make_async_remote_copy(
            src_ref=dst, dst_ref=dst, send_sem=send_sems.at[sem], recv_sem=recv_sems.at[sem],
            device_id=dev(), device_id_type=MESH,
        ).wait_recv()

    own_rows = pl.ds(pl.multiple_of(ctx * ROWS, ROWS), ROWS)
    loads = [
        pltpu.make_async_copy(src, dst, in_sems.at[i])
        for i, (src, dst) in enumerate(
            [(lc_in, lc), (qn_in, qn), (wk_in, wk), (og_in, og), (wv_in, wv), (qr_in, qr)]
        )
    ]
    for load in loads:
        load.start()
    partner = dev(core_to=1 - core)
    x_devs = [dev(dx=d) for d in range(1, 4)]
    y_devs = [dev(y_to=(y + d) % 4) for d in range(1, 4)]
    barrier = pltpu.get_barrier_semaphore()
    away = [(dy, other_l) for dy in range(4) for other_l in range(2)][1:]
    tp_devs = [dev(y_to=(y + dy) % 4, zl_to=(zl + other_l) % 2) for dy, other_l in away]
    z_devs = [dev(zh_to=(zh + d) % 4, zl_to=l) for d in range(1, 4) for l in range(2)]
    peers = tp_devs + [partner] + z_devs + x_devs
    for peer in peers:
        pl.semaphore_signal(barrier, inc=1, device_id=peer, device_id_type=MESH)
    loads[0].wait()
    whole = (
        lax.broadcasted_iota(jnp.int32, (ROWS, ROWS), 0) == lax.broadcasted_iota(jnp.int32, (ROWS, ROWS), 1)
    ).astype(F32).astype(BF16)
    cache[own_rows, :] = dot_nt(whole, lc[...]).astype(BF16)
    pl.semaphore_wait(barrier, len(peers))

    outward = zl * 2 - 1
    zh_of = [zh, (zh + outward + 4) % 4, (zh - outward + 4) % 4, (zh + 2) % 4]
    own_start = core * 64 + parity * 32
    mate_start = core * 64 + (1 - parity) * 32

    def at_x(d):
        return (x + d) % 4

    def chunk(dx, j, start, rows=32):
        block = at_x(dx) * 4 + zh_of[j]
        return cache.at[pl.ds(pl.multiple_of(block * ROWS + start, 16), rows), :]

    def sem_grid(rows, cols):
        return [[new_sem() for _ in range(cols)] for _ in range(rows)]

    z_sem = sem_grid(1, 4)[0]
    x_sem, ym_sem, yp_sem, core_sem, mate_sem = (sem_grid(4, 4) for _ in range(5))

    def same(ref, sem, to):
        send(ref, ref, sem, to)

    def along_x(j):
        for d in (2, 1, 3):
            same(chunk(0, j, own_start), x_sem[4 - d][j], x_devs[d - 1])

    def share(dx, j):
        same(chunk(dx, j, own_start, 16), ym_sem[dx][j], y_devs[0])
        same(chunk(dx, j, own_start + 16, 16), yp_sem[dx][j], y_devs[2])
        same(chunk(dx, j, own_start), core_sem[dx][j], partner)

    def from_z(j):
        arrived(chunk(0, j, own_start), z_sem[j])
        along_x(j)
        share(0, j)

    def from_x(j):
        for dx in (1, 3, 2):
            arrived(chunk(dx, j, own_start), x_sem[dx][j])
            share(dx, j)

    def from_y(dx, j):
        arrived(chunk(dx, j, mate_start, 16), ym_sem[dx][j])
        arrived(chunk(dx, j, mate_start + 16, 16), yp_sem[dx][j])
        same(chunk(dx, j, mate_start), mate_sem[dx][j], partner)

    def from_core(dx, j):
        arrived(chunk(dx, j, (1 - core) * 64 + parity * 32), core_sem[dx][j])
        arrived(chunk(dx, j, (1 - core) * 64 + (1 - parity) * 32), mate_sem[dx][j])

    same(chunk(0, 0, own_start), z_sem[1], dev(zh_to=zh_of[1], zl_to=1 - zl))
    same(chunk(0, 0, own_start), z_sem[2], dev(zh_to=zh_of[1]))
    same(chunk(0, 0, own_start), z_sem[3], dev(zh_to=zh_of[3], zl_to=1 - zl))
    along_x(0)

    for load in loads[1:]:
        load.wait()
    position = ctx * ROWS + lax.broadcasted_iota(jnp.int32, (1, ROWS), 1)
    kept = (mask_ref[...] == 1) & (position >= bound_ref[0])
    diagonal = lax.broadcasted_iota(jnp.int32, (ROWS, ROWS), 0) == lax.broadcasted_iota(
        jnp.int32, (ROWS, ROWS), 1
    )
    keep = jnp.where(diagonal & kept, 1.0, 0.0).astype(BF16)
    cot[...] = dot(keep, og[...]).astype(BF16)
    eye = (
        lax.broadcasted_iota(jnp.int32, (ROPE, ROPE), 0)
        == lax.broadcasted_iota(jnp.int32, (ROPE, ROPE), 1)
    ).astype(F32).astype(BF16)
    q_rows[T:, LATENT:] = jnp.zeros((T, ROPE), BF16)
    def products(h):
        cols = slice(h * 128, (h + 1) * 128)
        low = slice(T + h * 128, T + (h + 1) * 128)
        q_rows[cols, :LATENT] = (dot_nt(qn[:, cols], wk[:, cols]) * TO_BASE2).astype(BF16)
        q_cols[:LATENT, cols] = (dot_nt(wk[:, cols], qn[:, cols]) * TO_BASE2).astype(BF16)
        rope = (qr[:, h * ROPE:(h + 1) * ROPE].astype(F32) * TO_BASE2).astype(BF16)
        q_rows[cols, LATENT:] = rope
        q_cols[LATENT:, cols] = dot_nt(eye, rope).astype(BF16)
        q_rows[low, :LATENT] = dot_nt(cot[:, cols], wv[:, cols]).astype(BF16)
        q_cols[:LATENT, low] = dot_nt(wv[:, cols], cot[:, cols]).astype(BF16)

    def group(j, first):
        blocks = [pl.ds(pl.multiple_of((xb * 4 + zh_of[j]) * ROWS, ROWS), ROWS) for xb in range(4)]
        rows = slice(j * 512, (j + 1) * 512)

        for c in range(2):
            s_cols = slice(c * 256, (c + 1) * 256)
            p_cols = slice(T + c * 256, T + (c + 1) * 256)
            part = jnp.concatenate([cache[block, :] for block in blocks], axis=0)
            s = dot(part, q_cols[:, s_cols])
            dp = dot(part[:, :LATENT], q_cols[:LATENT, p_cols])
            dp_buf[rows, s_cols] = dp
            top = jnp.max(s, axis=0, keepdims=True)
            if not first:
                top = jnp.maximum(top, m_run[:, s_cols])
            e = jnp.exp2(s - top)
            e_buf[rows, s_cols] = e
            total = jnp.sum(e, axis=0, keepdims=True)
            weighted = jnp.sum(e * dp, axis=0, keepdims=True)
            if not first:
                shrink = jnp.exp2(m_run[:, s_cols] - top)
                total = total + l_run[:, s_cols] * shrink
                weighted = weighted + d_run[:, s_cols] * shrink
            m_run[:, s_cols] = top
            l_run[:, s_cols] = total
            d_run[:, s_cols] = weighted
            m_at[j, :, s_cols] = top

    def turn(j):
        for xb in range(4):
            block = pl.ds(pl.multiple_of((xb * 4 + zh_of[j]) * ROWS, ROWS), ROWS)
            cols = slice(j * 512 + xb * ROWS, j * 512 + (xb + 1) * ROWS)
            cache_t[:LATENT, cols] = cache[block, :LATENT].T
            cache_t[LATENT:, cols] = dot_nt(eye, cache[block, LATENT:]).astype(BF16)

    products(0)
    products(1)
    from_z(1)
    products(2)
    from_z(2)
    products(3)
    from_x(0)
    from_z(3)
    from_x(1)
    for j in range(1, 4):
        from_y(0, j)
    for dx in range(1, 4):
        from_y(dx, 0)
    for dx in range(1, 4):
        from_core(dx, 0)
    group(0, True)
    turn(0)
    from_x(2)
    for dx in range(1, 4):
        from_y(dx, 1)
    from_x(3)
    for dx in range(4):
        from_core(dx, 1)
    group(1, False)
    turn(1)
    for j in (2, 3):
        for dx in range(1, 4):
            from_y(dx, j)
    for dx in range(4):
        from_core(dx, 2)
    group(2, False)
    turn(2)
    for dx in range(4):
        from_core(dx, 3)
    group(3, False)

    l_run[...] = 1.0 / l_run[...]
    d_run[...] = d_run[...] * l_run[...]
    d_sem = sem_grid(1, 4)[0]
    y_sem, xr_sem = sem_grid(4, 3), sem_grid(4, 3)
    zz_sem, side_z_sem = sem_grid(1, 4)[0], sem_grid(4, 2)
    side_x_sem = sem_grid(1, 3)[0]
    main_sem, side_sem = sem_grid(1, 7)[0], sem_grid(1, 7)[0]
    wx_sem, wz_sem = sem_grid(4, 3), sem_grid(4, 3)

    def probabilities(j):
        weight = jnp.exp2(m_at[j] - m_run[...]) * l_run[...]
        delta = d_run[...]
        for i in range(16):
            part = slice(j * 512 + i * 32, j * 512 + (i + 1) * 32)
            p = e_buf[part, :] * weight
            ds_p[part, T:] = p.astype(BF16)
            ds_p[part, :T] = (p * (dp_buf[part, :] - delta) * LN2).astype(BF16)

    def cache_terms(j):
        terms = dot(ds_p[j * 512:(j + 1) * 512, :], q_rows[...])
        d_buf[j] = terms.astype(BF16).reshape(4, ROWS, CACHE)
        send(
            d_buf.at[j, :, pl.ds(pl.multiple_of((1 - core) * 64, 64), 64), :],
            d_recv.at[j], d_sem[j], partner,
        )

    def y_rows(d):
        return pl.ds(pl.multiple_of(((y + d) % 4) * 16, 16), 16)

    def l_rows(l):
        return pl.ds(pl.multiple_of(l * 32, 32), 32)

    def pair_sum(j):
        arrived(d_recv.at[j], d_sem[j])

        def block(b, carry):
            own = d_buf[j, b, pl.ds(pl.multiple_of(core * 64, 64), 64), :]
            total = (own.astype(F32) + d_recv[j, b].astype(F32)).astype(BF16)
            a_buf[j, b] = total[:, :MAIN]
            s_buf[j, b] = total[:, MAIN:]
            return carry

        lax.fori_loop(0, 4, block, 0)
        for d in (2, 1, 3):
            send(a_buf.at[j, :, y_rows(d), :], y_recv.at[j, d - 1], y_sem[j][d - 1], y_devs[d - 1])
        send(s_buf.at[j, :, l_rows(1 - zl), :], side_recv.at[j, 1], side_z_sem[j][1], dev(zh_to=zh_of[j], zl_to=1 - zl))
        if j > 0:
            send(s_buf.at[j, :, l_rows(zl), :], side_recv.at[j, 0], side_z_sem[j][0], dev(zh_to=zh_of[j]))

    def y_sum(j):
        for d in range(3):
            arrived(y_recv.at[j, d], y_sem[j][d])

        def block(b, carry):
            total = a_buf[j, b, y_rows(0), :].astype(F32)
            for d in range(3):
                total = total + y_recv[j, d, b].astype(F32)
            a2_buf[j, b] = total.astype(BF16)
            return carry

        lax.fori_loop(0, 4, block, 0)
        for d in (2, 1, 3):
            send(a2_buf.at[j, at_x(d)], x_recv.at[j, d - 1], xr_sem[j][d - 1], x_devs[d - 1])

    def x_sum(j):
        for d in range(3):
            arrived(x_recv.at[j, d], xr_sem[j][d])
        total = a2_buf[j, x].astype(F32)
        for d in range(3):
            total = total + x_recv[j, d].astype(F32)
        a3_buf[j] = total.astype(BF16)
        if j > 0:
            send(a3_buf.at[j], z_recv.at[j], zz_sem[j], dev(zh_to=zh_of[j]))

    def side_z_sum():
        slots = [(j, other) for j in (3, 1, 2, 0) for other in range(2) if j > 0 or other]
        for j, other in slots:
            arrived(side_recv.at[j, other], side_z_sem[j][other])

        def block(b, carry):
            total = s_buf[0, b, l_rows(zl), :].astype(F32)
            for j, other in slots:
                total = total + side_recv[j, other, b].astype(F32)
            sx_buf[b] = total.astype(BF16)
            return carry

        lax.fori_loop(0, 4, block, 0)
        for d in (2, 1, 3):
            send(sx_buf.at[at_x(d)], sx_recv.at[d - 1], side_x_sem[d - 1], x_devs[d - 1])

    def side_x_sum():
        for d in range(3):
            arrived(sx_recv.at[d], side_x_sem[d])
        total = sx_buf[x].astype(F32)
        for d in range(3):
            total = total + sx_recv[d].astype(F32)
        side = side_share(0, 0)
        side[...] = total.astype(BF16)
        for i, to in enumerate(tp_devs):
            same(side, side_sem[i], to)

    def z_sum():
        total = a3_buf[0].astype(F32)
        for j in (3, 1, 2):
            arrived(z_recv.at[j], zz_sem[j])
            total = total + z_recv[j].astype(F32)
        main = main_share(0, 0)
        main[...] = total.astype(BF16)
        for i, to in enumerate(tp_devs):
            same(main, main_sem[i], to)

    def main_share(dy, other_l):
        rows = pl.ds(pl.multiple_of((y + dy) % 4 * 16, 16), 16)
        return g_main.at[(zl + other_l) % 2, rows, :]

    def side_share(dy, other_l):
        return g_side.at[(y + dy) % 4, l_rows((zl + other_l) % 2), :]

    def latent_out(c):
        cols = slice(c * 256, (c + 1) * 256)
        part = dot(cache_t[...], ds_p[:, cols])
        acc[:, cols] = part
        og_t[:, cols] = part.astype(BF16)
        for i in range(2):
            at = slice(c * 256 + i * 128, c * 256 + (i + 1) * 128)
            heads = slice((c % 2) * 256 + i * 128, (c % 2) * 256 + (i + 1) * 128)
            rows = qn[:, heads] if c < 2 else cot[:, heads]
            terms = dot(og_t[:LATENT, at], rows) * (TO_BASE2 if c < 2 else 1.0)
            w_buf[c, :, :, i * 128:(i + 1) * 128] = terms.astype(BF16).reshape(4, 128, 128)

    def w_send(c):
        for d in (2, 1, 3):
            send(w_buf.at[c, at_x(d)], w_xrecv.at[c, d - 1], wx_sem[c][d - 1], x_devs[d - 1])

    def w_rows(d):
        return pl.ds(pl.multiple_of(((zh + d) % 4) * 32, 32), 32)

    def w_x_sum(c):
        for d in range(3):
            arrived(w_xrecv.at[c, d], wx_sem[c][d])
        total = w_buf[c, x].astype(F32)
        for d in range(3):
            total = total + w_xrecv[c, d].astype(F32)
        w2_buf[c] = total.astype(BF16)
        for d in (2, 1, 3):
            send(w2_buf.at[c, w_rows(d), :], w_zrecv.at[c, d - 1], wz_sem[c][d - 1], dev(zh_to=(zh + d) % 4))

    def w_z_sum(c):
        for d in range(3):
            arrived(w_zrecv.at[c, d], wz_sem[c][d])
        total = w2_buf[c, w_rows(0), :].astype(F32)
        for d in range(3):
            total = total + w_zrecv[c, d].astype(F32)
        ref = gwk_ref if c < 2 else gwv_ref
        ref[:, (c % 2) * 256:(c % 2 + 1) * 256] = total

    def outputs(h):
        cols = slice(h * 128, (h + 1) * 128)
        low = slice(T + h * 128, T + (h + 1) * 128)
        out_ref[:, cols] = dot_tn(og_t[:LATENT, low], wv[:, cols]).astype(BF16)
        gqn_ref[:, cols] = (dot_tn(og_t[:LATENT, cols], wk[:, cols]) * TO_BASE2).astype(BF16)
        gqr_ref[:, h * ROPE:(h + 1) * ROPE] = (acc[LATENT:, cols].T * TO_BASE2).astype(BF16)

    stores = []

    def store(src, dst):
        copy = pltpu.make_async_copy(src, dst, out_sems.at[len(stores)])
        copy.start()
        stores.append(copy)

    probabilities(3)
    cache_terms(3)
    probabilities(1)
    cache_terms(1)
    pair_sum(3)
    probabilities(2)
    cache_terms(2)
    pair_sum(1)
    probabilities(0)
    cache_terms(0)
    turn(3)
    latent_out(0)
    w_send(0)
    pair_sum(2)
    pair_sum(0)
    latent_out(2)
    w_send(2)
    y_sum(3)
    latent_out(1)
    y_sum(1)
    latent_out(3)
    y_sum(2)
    w_send(1)
    for h in range(HEADS):
        outputs(h)
    store(out_ref, out_to)
    store(gqn_ref, gqn_to)
    store(gqr_ref, gqr_to)
    w_x_sum(0)
    y_sum(0)
    side_z_sum()
    w_send(3)
    x_sum(3)
    x_sum(1)
    w_x_sum(2)
    x_sum(2)
    x_sum(0)
    side_x_sum()
    z_sum()
    w_x_sum(1)
    w_x_sum(3)
    for i, (dy, other_l) in enumerate(away):
        arrived(main_share((4 - dy) % 4, other_l), main_sem[i])
        arrived(side_share((4 - dy) % 4, other_l), side_sem[i])
    own_half = pl.ds(pl.multiple_of(core * 64, 64), 64)
    mate_half = pl.ds(pl.multiple_of((1 - core) * 64, 64), 64)
    gather[own_half, :MAIN] = (g_main[0].astype(F32) + g_main[1].astype(F32)).astype(BF16)
    total = g_side[0].astype(F32)
    for i in range(1, 4):
        total = total + g_side[i].astype(F32)
    gather[own_half, MAIN:] = total.astype(BF16)
    half_sem = new_sem()
    same(gather.at[own_half, :], half_sem, partner)
    for c in (0, 2, 1, 3):
        w_z_sum(c)
    store(gwk_ref, gwk_to)
    store(gwv_ref, gwv_to)
    arrived(gather.at[mate_half, :], half_sem)
    store(gather, glat_to)
    for copy in stores:
        copy.wait()
    for copy in sent:
        copy.wait_send()
    assert counter[0] <= N_SEMS


def hand_over(lat_in, *refs):
    ins, lat_out, outs = refs[:5], refs[5], refs[6:11]
    for source, target in zip(ins, outs):
        target[...] = source[...]
    lat_out[...] = lat_in[...].astype(F32).T


def per_device(
    query_nope, query_rope, latent_cache, up_keys, up_values, out_grad, response_mask, boundary
):
    anywhere = pl.BlockSpec(memory_space=pl.ANY)
    vmem = pl.BlockSpec(memory_space=pltpu.VMEM)
    scratch = [
        ((CACHE, ROWS), BF16),
        ((ROWS, T), BF16), ((ROWS, HEADS * ROPE), BF16), ((LATENT, T), BF16), ((LATENT, T), BF16),
        ((ROWS, T), BF16), ((ROWS, T), BF16),
        ((SEQ, CACHE), BF16), ((CACHE, SEQ), BF16),
        ((2 * T, CACHE), BF16), ((CACHE, 2 * T), BF16),
        ((SEQ, T), F32), ((SEQ, T), F32),
        ((1, T), F32), ((1, T), F32), ((1, T), F32), ((4, 1, T), F32),
        ((SEQ, 2 * T), BF16),
        ((CACHE, 2 * T), F32), ((CACHE, 2 * T), BF16),
        ((4, 4, 64, SIDE), BF16), ((4, 2, 4, 32, SIDE), BF16), ((4, 32, SIDE), BF16),
        ((3, 32, SIDE), BF16), ((2, 64, MAIN), BF16), ((4, 64, SIDE), BF16),
        ((4, 4, ROWS, CACHE), BF16), ((4, 4, 64, CACHE), BF16), ((4, 4, 64, MAIN), BF16),
        ((4, 3, 4, 16, MAIN), BF16), ((4, 4, 16, MAIN), BF16), ((4, 3, 16, MAIN), BF16),
        ((4, 16, MAIN), BF16), ((4, 16, MAIN), BF16), ((ROWS, CACHE), BF16),
        ((4, 4, 128, 256), BF16), ((4, 3, 128, 256), BF16), ((4, 128, 256), BF16), ((4, 3, 32, 256), BF16),
        ((ROWS, T), BF16), ((ROWS, T), BF16), ((ROWS, HEADS * ROPE), BF16), ((32, T), F32), ((32, T), F32),
    ]
    results = pl.pallas_call(
        kernel,
        out_shape=(
            jax.ShapeDtypeStruct((ROWS, HEADS * VDIM), BF16),
            jax.ShapeDtypeStruct((ROWS, HEADS * NOPE), BF16),
            jax.ShapeDtypeStruct((ROWS, HEADS * ROPE), BF16),
            jax.ShapeDtypeStruct((ROWS, CACHE), BF16),
            jax.ShapeDtypeStruct((32, HEADS * NOPE), F32),
            jax.ShapeDtypeStruct((32, HEADS * VDIM), F32),
        ),
        in_specs=[anywhere] * 6 + [vmem, pl.BlockSpec(memory_space=pltpu.SMEM)],
        out_specs=(anywhere,) * 6,
        scratch_shapes=[pltpu.VMEM(shape, dtype) for shape, dtype in scratch]
        + [
            pltpu.SemaphoreType.DMA((6,)),
            pltpu.SemaphoreType.DMA((6,)),
            pltpu.SemaphoreType.DMA((N_SEMS,)),
            pltpu.SemaphoreType.DMA((N_SEMS,)),
        ],
        compiler_params=pltpu.CompilerParams(
            collective_id=0, has_side_effects=True, vmem_limit_bytes=56 * 1024 * 1024
        ),
        cost_estimate=pl.CostEstimate(flops=8 * 10**9, bytes_accessed=4 * 10**6, transcendentals=10**6),
    )(
        query_nope, query_rope, latent_cache.T, up_keys, up_values, out_grad,
        response_mask.reshape(1, ROWS), boundary,
    )
    order = (3, 0, 1, 2, 4, 5)
    handed = pl.pallas_call(
        hand_over,
        out_shape=(jax.ShapeDtypeStruct((CACHE, ROWS), F32),)
        + tuple(jax.ShapeDtypeStruct(results[i].shape, results[i].dtype) for i in order[1:]),
        in_specs=[vmem] * 6,
        out_specs=(vmem,) * 6,
    )(*[results[i] for i in order])
    return (handed[1], handed[2], handed[3], handed[0].T, handed[4], handed[5])


def solution(mesh):
    in_specs = (
        P("ctx", "tp"),
        P("ctx", "tp"),
        P("ctx", None),
        P(None, "tp"),
        P(None, "tp"),
        P("ctx", "tp"),
        P("ctx"),
        P(),
    )
    out_specs = (
        P("ctx", "tp"),
        P("ctx", "tp"),
        P("ctx", "tp"),
        P("ctx", None),
        P("ctx", "tp"),
        P("ctx", "tp"),
    )
    return jax.shard_map(
        per_device, mesh=mesh, in_specs=in_specs, out_specs=out_specs, check_vma=False
    )
```

```python
import math

import jax
import jax.numpy as jnp
from jax import lax
from jax.experimental import pallas as pl
from jax.experimental.pallas import tpu as pltpu
from jax.sharding import PartitionSpec as P

LATENT = 512
ROPE = 64
CACHE = LATENT + ROPE
NOPE = 128
VDIM = 128
ROWS = 128
HEADS = 4
SEQ = 2048
T = HEADS * ROWS
SCALE = 1.0 / math.sqrt(NOPE + ROPE)
TO_BASE2 = SCALE / math.log(2.0)
MAIN = 384
SIDE = CACHE - MAIN
MESH = pl.DeviceIdType.MESH
BF16 = jnp.bfloat16
F32 = jnp.float32
N_SEMS = 208


def dot(a, b):
    return jnp.dot(a, b, preferred_element_type=F32)


def dot_nt(a, b):
    return lax.dot_general(a, b, (((1,), (1,)), ((), ())), preferred_element_type=F32)


def dot_tn(a, b):
    return lax.dot_general(a, b, (((0,), (0,)), ((), ())), preferred_element_type=F32)


def kernel(
    qn_in, qr_in, lc_in, wk_in, wv_in, og_in, mask_ref, bound_ref,
    out_to, gqn_to, gqr_to, glat_to, gwk_to, gwv_to,
    lc, qn, qr, wk, wv, og, cot, cache, cache_t, q_rows, q_cols,
    e_buf, dp_buf, m_run, l_run, d_run, m_at, ds_p, acc, og_t,
    s_buf, side_recv, sx_buf, sx_recv, g_main, g_side,
    d_buf, d_recv, a_buf, y_recv, a2_buf, x_recv, a3_buf, z_recv, gather,
    w_buf, w_xrecv, w2_buf, w_zrecv,
    out_ref, gqn_ref, gqr_ref, gwk_ref, gwv_ref,
    in_sems, out_sems, send_sems, recv_sems,
):
    ctx, tp = lax.axis_index("ctx"), lax.axis_index("tp")
    x, zh = ctx // 4, ctx % 4
    y, zl, core = tp // 4, (tp // 2) % 2, tp % 2
    parity = y % 2

    def dev(dx=0, zh_to=None, y_to=None, zl_to=None, core_to=None):
        to_x = (x + dx) % 4
        to_zh = zh if zh_to is None else zh_to
        to_y = y if y_to is None else y_to
        to_zl = zl if zl_to is None else zl_to
        to_core = core if core_to is None else core_to
        return (to_x * 4 + to_zh, to_y * 4 + to_zl * 2 + to_core)

    counter = [0]
    sent = []

    def new_sem():
        counter[0] += 1
        return counter[0] - 1

    def send(src, dst, sem, to):
        copy = pltpu.make_async_remote_copy(
            src_ref=src, dst_ref=dst, send_sem=send_sems.at[sem], recv_sem=recv_sems.at[sem],
            device_id=to, device_id_type=MESH,
        )
        copy.start()
        sent.append(copy)

    def arrived(dst, sem):
        pltpu.make_async_remote_copy(
            src_ref=dst, dst_ref=dst, send_sem=send_sems.at[sem], recv_sem=recv_sems.at[sem],
            device_id=dev(), device_id_type=MESH,
        ).wait_recv()

    own_rows = pl.ds(pl.multiple_of(ctx * ROWS, ROWS), ROWS)
    loads = [
        pltpu.make_async_copy(src, dst, in_sems.at[i])
        for i, (src, dst) in enumerate(
            [(lc_in, lc), (qn_in, qn), (wk_in, wk), (og_in, og), (wv_in, wv), (qr_in, qr)]
        )
    ]
    for load in loads:
        load.start()
    partner = dev(core_to=1 - core)
    x_devs = [dev(dx=d) for d in range(1, 4)]
    y_devs = [dev(y_to=(y + d) % 4) for d in range(1, 4)]
    barrier = pltpu.get_barrier_semaphore()
    away = [(dy, other_l) for dy in range(4) for other_l in range(2)][1:]
    tp_devs = [dev(y_to=(y + dy) % 4, zl_to=(zl + other_l) % 2) for dy, other_l in away]
    z_devs = [dev(zh_to=(zh + d) % 4, zl_to=l) for d in range(1, 4) for l in range(2)]
    peers = tp_devs + [partner] + z_devs + x_devs
    for peer in peers:
        pl.semaphore_signal(barrier, inc=1, device_id=peer, device_id_type=MESH)
    loads[0].wait()
    whole = (
        lax.broadcasted_iota(jnp.int32, (ROWS, ROWS), 0) == lax.broadcasted_iota(jnp.int32, (ROWS, ROWS), 1)
    ).astype(F32).astype(BF16)
    cache[own_rows, :] = dot_nt(whole, lc[...]).astype(BF16)
    pl.semaphore_wait(barrier, len(peers))

    outward = zl * 2 - 1
    zh_of = [zh, (zh + outward + 4) % 4, (zh - outward + 4) % 4, (zh + 2) % 4]
    own_start = core * 64 + parity * 32
    mate_start = core * 64 + (1 - parity) * 32

    def at_x(d):
        return (x + d) % 4

    def chunk(dx, j, start, rows=32):
        block = at_x(dx) * 4 + zh_of[j]
        return cache.at[pl.ds(pl.multiple_of(block * ROWS + start, 16), rows), :]

    def sem_grid(rows, cols):
        return [[new_sem() for _ in range(cols)] for _ in range(rows)]

    z_sem = sem_grid(1, 4)[0]
    x_sem, ym_sem, yp_sem, core_sem, mate_sem = (sem_grid(4, 4) for _ in range(5))

    def same(ref, sem, to):
        send(ref, ref, sem, to)

    def along_x(j):
        for d in (2, 1, 3):
            same(chunk(0, j, own_start), x_sem[4 - d][j], x_devs[d - 1])

    def share(dx, j):
        same(chunk(dx, j, own_start, 16), ym_sem[dx][j], y_devs[0])
        same(chunk(dx, j, own_start + 16, 16), yp_sem[dx][j], y_devs[2])
        same(chunk(dx, j, own_start), core_sem[dx][j], partner)

    def from_z(j):
        arrived(chunk(0, j, own_start), z_sem[j])
        along_x(j)
        share(0, j)

    def from_x(j):
        for dx in (1, 3, 2):
            arrived(chunk(dx, j, own_start), x_sem[dx][j])
            share(dx, j)

    def from_y(dx, j):
        arrived(chunk(dx, j, mate_start, 16), ym_sem[dx][j])
        arrived(chunk(dx, j, mate_start + 16, 16), yp_sem[dx][j])
        same(chunk(dx, j, mate_start), mate_sem[dx][j], partner)

    def from_core(dx, j):
        arrived(chunk(dx, j, (1 - core) * 64 + parity * 32), core_sem[dx][j])
        arrived(chunk(dx, j, (1 - core) * 64 + (1 - parity) * 32), mate_sem[dx][j])

    same(chunk(0, 0, own_start), z_sem[1], dev(zh_to=zh_of[1], zl_to=1 - zl))
    same(chunk(0, 0, own_start), z_sem[2], dev(zh_to=zh_of[1]))
    same(chunk(0, 0, own_start), z_sem[3], dev(zh_to=zh_of[3], zl_to=1 - zl))
    along_x(0)

    for load in loads[1:]:
        load.wait()
    position = ctx * ROWS + lax.broadcasted_iota(jnp.int32, (1, ROWS), 1)
    kept = (mask_ref[...] == 1) & (position >= bound_ref[0])
    diagonal = lax.broadcasted_iota(jnp.int32, (ROWS, ROWS), 0) == lax.broadcasted_iota(
        jnp.int32, (ROWS, ROWS), 1
    )
    keep = jnp.where(diagonal & kept, 1.0, 0.0).astype(BF16)
    cot[...] = dot(keep, og[...]).astype(BF16)
    eye = (
        lax.broadcasted_iota(jnp.int32, (ROPE, ROPE), 0)
        == lax.broadcasted_iota(jnp.int32, (ROPE, ROPE), 1)
    ).astype(F32).astype(BF16)
    q_rows[T:, LATENT:] = jnp.zeros((T, ROPE), BF16)
    def products(h):
        cols = slice(h * 128, (h + 1) * 128)
        low = slice(T + h * 128, T + (h + 1) * 128)
        q_rows[cols, :LATENT] = dot_nt(qn[:, cols], wk[:, cols]).astype(BF16)
        q_cols[:LATENT, cols] = dot_nt(wk[:, cols], qn[:, cols]).astype(BF16)
        rope = qr[:, h * ROPE:(h + 1) * ROPE]
        q_rows[cols, LATENT:] = rope
        q_cols[LATENT:, cols] = dot_nt(eye, rope).astype(BF16)
        q_rows[low, :LATENT] = dot_nt(cot[:, cols], wv[:, cols]).astype(BF16)
        q_cols[:LATENT, low] = dot_nt(wv[:, cols], cot[:, cols]).astype(BF16)

    def group(j, first):
        blocks = [pl.ds(pl.multiple_of((xb * 4 + zh_of[j]) * ROWS, ROWS), ROWS) for xb in range(4)]
        rows = slice(j * 512, (j + 1) * 512)

        for c in range(2):
            s_cols = slice(c * 256, (c + 1) * 256)
            p_cols = slice(T + c * 256, T + (c + 1) * 256)
            part = jnp.concatenate([cache[block, :] for block in blocks], axis=0)
            s = dot(part, q_cols[:, s_cols]) * TO_BASE2
            dp = dot(part[:, :LATENT], q_cols[:LATENT, p_cols])
            dp_buf[rows, s_cols] = dp
            top = jnp.max(s, axis=0, keepdims=True)
            if not first:
                top = jnp.maximum(top, m_run[:, s_cols])
            e = jnp.exp2(s - top)
            e_buf[rows, s_cols] = e
            total = jnp.sum(e, axis=0, keepdims=True)
            weighted = jnp.sum(e * dp, axis=0, keepdims=True)
            if not first:
                shrink = jnp.exp2(m_run[:, s_cols] - top)
                total = total + l_run[:, s_cols] * shrink
                weighted = weighted + d_run[:, s_cols] * shrink
            m_run[:, s_cols] = top
            l_run[:, s_cols] = total
            d_run[:, s_cols] = weighted
            m_at[j, :, s_cols] = top

    def turn(j):
        for xb in range(4):
            block = pl.ds(pl.multiple_of((xb * 4 + zh_of[j]) * ROWS, ROWS), ROWS)
            cols = slice(j * 512 + xb * ROWS, j * 512 + (xb + 1) * ROWS)
            cache_t[:LATENT, cols] = cache[block, :LATENT].T
            cache_t[LATENT:, cols] = dot_nt(eye, cache[block, LATENT:]).astype(BF16)

    products(0)
    products(1)
    from_z(1)
    products(2)
    from_z(2)
    products(3)
    from_x(0)
    from_z(3)
    from_x(1)
    for j in range(1, 4):
        from_y(0, j)
    for dx in range(1, 4):
        from_y(dx, 0)
    for dx in range(1, 4):
        from_core(dx, 0)
    group(0, True)
    turn(0)
    from_x(2)
    for dx in range(1, 4):
        from_y(dx, 1)
    from_x(3)
    for dx in range(4):
        from_core(dx, 1)
    group(1, False)
    turn(1)
    for j in (2, 3):
        for dx in range(1, 4):
            from_y(dx, j)
    for dx in range(4):
        from_core(dx, 2)
    group(2, False)
    turn(2)
    for dx in range(4):
        from_core(dx, 3)
    group(3, False)

    l_run[...] = 1.0 / l_run[...]
    d_run[...] = d_run[...] * l_run[...]
    d_sem = sem_grid(1, 4)[0]
    y_sem, xr_sem = sem_grid(4, 3), sem_grid(4, 3)
    zz_sem, side_z_sem = sem_grid(1, 4)[0], sem_grid(4, 2)
    side_x_sem = sem_grid(1, 3)[0]
    main_sem, side_sem = sem_grid(1, 7)[0], sem_grid(1, 7)[0]
    wx_sem, wz_sem = sem_grid(4, 3), sem_grid(4, 3)

    def probabilities(j):
        weight = jnp.exp2(m_at[j] - m_run[...]) * l_run[...]
        delta = d_run[...]
        for i in range(16):
            part = slice(j * 512 + i * 32, j * 512 + (i + 1) * 32)
            p = e_buf[part, :] * weight
            ds_p[part, T:] = p.astype(BF16)
            ds_p[part, :T] = (p * (dp_buf[part, :] - delta) * SCALE).astype(BF16)

    def cache_terms(j):
        terms = dot(ds_p[j * 512:(j + 1) * 512, :], q_rows[...])
        d_buf[j] = terms.astype(BF16).reshape(4, ROWS, CACHE)
        send(
            d_buf.at[j, :, pl.ds(pl.multiple_of((1 - core) * 64, 64), 64), :],
            d_recv.at[j], d_sem[j], partner,
        )

    def y_rows(d):
        return pl.ds(pl.multiple_of(((y + d) % 4) * 16, 16), 16)

    def l_rows(l):
        return pl.ds(pl.multiple_of(l * 32, 32), 32)

    def pair_sum(j):
        arrived(d_recv.at[j], d_sem[j])

        def block(b, carry):
            own = d_buf[j, b, pl.ds(pl.multiple_of(core * 64, 64), 64), :]
            total = (own.astype(F32) + d_recv[j, b].astype(F32)).astype(BF16)
            a_buf[j, b] = total[:, :MAIN]
            s_buf[j, b] = total[:, MAIN:]
            return carry

        lax.fori_loop(0, 4, block, 0)
        for d in (2, 1, 3):
            send(a_buf.at[j, :, y_rows(d), :], y_recv.at[j, d - 1], y_sem[j][d - 1], y_devs[d - 1])
        send(s_buf.at[j, :, l_rows(1 - zl), :], side_recv.at[j, 1], side_z_sem[j][1], dev(zh_to=zh_of[j], zl_to=1 - zl))
        if j > 0:
            send(s_buf.at[j, :, l_rows(zl), :], side_recv.at[j, 0], side_z_sem[j][0], dev(zh_to=zh_of[j]))

    def y_sum(j):
        for d in range(3):
            arrived(y_recv.at[j, d], y_sem[j][d])

        def block(b, carry):
            total = a_buf[j, b, y_rows(0), :].astype(F32)
            for d in range(3):
                total = total + y_recv[j, d, b].astype(F32)
            a2_buf[j, b] = total.astype(BF16)
            return carry

        lax.fori_loop(0, 4, block, 0)
        for d in (2, 1, 3):
            send(a2_buf.at[j, at_x(d)], x_recv.at[j, d - 1], xr_sem[j][d - 1], x_devs[d - 1])

    def x_sum(j):
        for d in range(3):
            arrived(x_recv.at[j, d], xr_sem[j][d])
        total = a2_buf[j, x].astype(F32)
        for d in range(3):
            total = total + x_recv[j, d].astype(F32)
        a3_buf[j] = total.astype(BF16)
        if j > 0:
            send(a3_buf.at[j], z_recv.at[j], zz_sem[j], dev(zh_to=zh_of[j]))

    def side_z_sum():
        slots = [(j, other) for j in (3, 1, 2, 0) for other in range(2) if j > 0 or other]
        for j, other in slots:
            arrived(side_recv.at[j, other], side_z_sem[j][other])

        def block(b, carry):
            total = s_buf[0, b, l_rows(zl), :].astype(F32)
            for j, other in slots:
                total = total + side_recv[j, other, b].astype(F32)
            sx_buf[b] = total.astype(BF16)
            return carry

        lax.fori_loop(0, 4, block, 0)
        for d in (2, 1, 3):
            send(sx_buf.at[at_x(d)], sx_recv.at[d - 1], side_x_sem[d - 1], x_devs[d - 1])

    def side_x_sum():
        for d in range(3):
            arrived(sx_recv.at[d], side_x_sem[d])
        total = sx_buf[x].astype(F32)
        for d in range(3):
            total = total + sx_recv[d].astype(F32)
        side = side_share(0, 0)
        side[...] = total.astype(BF16)
        for i, to in enumerate(tp_devs):
            same(side, side_sem[i], to)

    def z_sum():
        total = a3_buf[0].astype(F32)
        for j in (3, 1, 2):
            arrived(z_recv.at[j], zz_sem[j])
            total = total + z_recv[j].astype(F32)
        main = main_share(0, 0)
        main[...] = total.astype(BF16)
        for i, to in enumerate(tp_devs):
            same(main, main_sem[i], to)

    def main_share(dy, other_l):
        rows = pl.ds(pl.multiple_of((y + dy) % 4 * 16, 16), 16)
        return g_main.at[(zl + other_l) % 2, rows, :]

    def side_share(dy, other_l):
        return g_side.at[(y + dy) % 4, l_rows((zl + other_l) % 2), :]

    def latent_out(c):
        cols = slice(c * 256, (c + 1) * 256)
        part = dot(cache_t[...], ds_p[:, cols])
        acc[:, cols] = part
        og_t[:, cols] = part.astype(BF16)
        for i in range(2):
            at = slice(c * 256 + i * 128, c * 256 + (i + 1) * 128)
            heads = slice((c % 2) * 256 + i * 128, (c % 2) * 256 + (i + 1) * 128)
            rows = qn[:, heads] if c < 2 else cot[:, heads]
            terms = dot(og_t[:LATENT, at], rows)
            w_buf[c, :, :, i * 128:(i + 1) * 128] = terms.astype(BF16).reshape(4, 128, 128)

    def w_send(c):
        for d in (2, 1, 3):
            send(w_buf.at[c, at_x(d)], w_xrecv.at[c, d - 1], wx_sem[c][d - 1], x_devs[d - 1])

    def w_rows(d):
        return pl.ds(pl.multiple_of(((zh + d) % 4) * 32, 32), 32)

    def w_x_sum(c):
        for d in range(3):
            arrived(w_xrecv.at[c, d], wx_sem[c][d])
        total = w_buf[c, x].astype(F32)
        for d in range(3):
            total = total + w_xrecv[c, d].astype(F32)
        w2_buf[c] = total.astype(BF16)
        for d in (2, 1, 3):
            send(w2_buf.at[c, w_rows(d), :], w_zrecv.at[c, d - 1], wz_sem[c][d - 1], dev(zh_to=(zh + d) % 4))

    def w_z_sum(c):
        for d in range(3):
            arrived(w_zrecv.at[c, d], wz_sem[c][d])
        total = w2_buf[c, w_rows(0), :].astype(F32)
        for d in range(3):
            total = total + w_zrecv[c, d].astype(F32)
        ref = gwk_ref if c < 2 else gwv_ref
        ref[:, (c % 2) * 256:(c % 2 + 1) * 256] = total

    def outputs(h):
        cols = slice(h * 128, (h + 1) * 128)
        low = slice(T + h * 128, T + (h + 1) * 128)
        out_ref[:, cols] = dot_tn(og_t[:LATENT, low], wv[:, cols]).astype(BF16)
        gqn_ref[:, cols] = dot_tn(og_t[:LATENT, cols], wk[:, cols]).astype(BF16)
        gqr_ref[:, h * ROPE:(h + 1) * ROPE] = acc[LATENT:, cols].T.astype(BF16)

    stores = []

    def store(src, dst):
        copy = pltpu.make_async_copy(src, dst, out_sems.at[len(stores)])
        copy.start()
        stores.append(copy)

    probabilities(3)
    cache_terms(3)
    probabilities(1)
    cache_terms(1)
    pair_sum(3)
    probabilities(2)
    cache_terms(2)
    pair_sum(1)
    probabilities(0)
    cache_terms(0)
    turn(3)
    latent_out(0)
    w_send(0)
    pair_sum(2)
    pair_sum(0)
    latent_out(2)
    w_send(2)
    y_sum(3)
    latent_out(1)
    y_sum(1)
    latent_out(3)
    y_sum(2)
    w_send(1)
    for h in range(HEADS):
        outputs(h)
    store(out_ref, out_to)
    store(gqn_ref, gqn_to)
    store(gqr_ref, gqr_to)
    w_x_sum(0)
    y_sum(0)
    side_z_sum()
    w_send(3)
    x_sum(3)
    x_sum(1)
    w_x_sum(2)
    x_sum(2)
    x_sum(0)
    side_x_sum()
    z_sum()
    w_x_sum(1)
    w_x_sum(3)
    for i, (dy, other_l) in enumerate(away):
        arrived(main_share((4 - dy) % 4, other_l), main_sem[i])
        arrived(side_share((4 - dy) % 4, other_l), side_sem[i])
    own_half = pl.ds(pl.multiple_of(core * 64, 64), 64)
    mate_half = pl.ds(pl.multiple_of((1 - core) * 64, 64), 64)
    gather[own_half, :MAIN] = (g_main[0].astype(F32) + g_main[1].astype(F32)).astype(BF16)
    total = g_side[0].astype(F32)
    for i in range(1, 4):
        total = total + g_side[i].astype(F32)
    gather[own_half, MAIN:] = total.astype(BF16)
    half_sem = new_sem()
    same(gather.at[own_half, :], half_sem, partner)
    for c in (0, 2, 1, 3):
        w_z_sum(c)
    store(gwk_ref, gwk_to)
    store(gwv_ref, gwv_to)
    arrived(gather.at[mate_half, :], half_sem)
    store(gather, glat_to)
    for copy in stores:
        copy.wait()
    for copy in sent:
        copy.wait_send()
    assert counter[0] <= N_SEMS


def hand_over(lat_in, *refs):
    ins, lat_out, outs = refs[:5], refs[5], refs[6:11]
    for source, target in zip(ins, outs):
        target[...] = source[...]
    lat_out[...] = lat_in[...].astype(F32).T


def per_device(
    query_nope, query_rope, latent_cache, up_keys, up_values, out_grad, response_mask, boundary
):
    anywhere = pl.BlockSpec(memory_space=pl.ANY)
    vmem = pl.BlockSpec(memory_space=pltpu.VMEM)
    scratch = [
        ((CACHE, ROWS), BF16),
        ((ROWS, T), BF16), ((ROWS, HEADS * ROPE), BF16), ((LATENT, T), BF16), ((LATENT, T), BF16),
        ((ROWS, T), BF16), ((ROWS, T), BF16),
        ((SEQ, CACHE), BF16), ((CACHE, SEQ), BF16),
        ((2 * T, CACHE), BF16), ((CACHE, 2 * T), BF16),
        ((SEQ, T), F32), ((SEQ, T), F32),
        ((1, T), F32), ((1, T), F32), ((1, T), F32), ((4, 1, T), F32),
        ((SEQ, 2 * T), BF16),
        ((CACHE, 2 * T), F32), ((CACHE, 2 * T), BF16),
        ((4, 4, 64, SIDE), BF16), ((4, 2, 4, 32, SIDE), BF16), ((4, 32, SIDE), BF16),
        ((3, 32, SIDE), BF16), ((2, 64, MAIN), BF16), ((4, 64, SIDE), BF16),
        ((4, 4, ROWS, CACHE), BF16), ((4, 4, 64, CACHE), BF16), ((4, 4, 64, MAIN), BF16),
        ((4, 3, 4, 16, MAIN), BF16), ((4, 4, 16, MAIN), BF16), ((4, 3, 16, MAIN), BF16),
        ((4, 16, MAIN), BF16), ((4, 16, MAIN), BF16), ((ROWS, CACHE), BF16),
        ((4, 4, 128, 256), BF16), ((4, 3, 128, 256), BF16), ((4, 128, 256), BF16), ((4, 3, 32, 256), BF16),
        ((ROWS, T), BF16), ((ROWS, T), BF16), ((ROWS, HEADS * ROPE), BF16), ((32, T), F32), ((32, T), F32),
    ]
    results = pl.pallas_call(
        kernel,
        out_shape=(
            jax.ShapeDtypeStruct((ROWS, HEADS * VDIM), BF16),
            jax.ShapeDtypeStruct((ROWS, HEADS * NOPE), BF16),
            jax.ShapeDtypeStruct((ROWS, HEADS * ROPE), BF16),
            jax.ShapeDtypeStruct((ROWS, CACHE), BF16),
            jax.ShapeDtypeStruct((32, HEADS * NOPE), F32),
            jax.ShapeDtypeStruct((32, HEADS * VDIM), F32),
        ),
        in_specs=[anywhere] * 6 + [vmem, pl.BlockSpec(memory_space=pltpu.SMEM)],
        out_specs=(anywhere,) * 6,
        scratch_shapes=[pltpu.VMEM(shape, dtype) for shape, dtype in scratch]
        + [
            pltpu.SemaphoreType.DMA((6,)),
            pltpu.SemaphoreType.DMA((6,)),
            pltpu.SemaphoreType.DMA((N_SEMS,)),
            pltpu.SemaphoreType.DMA((N_SEMS,)),
        ],
        compiler_params=pltpu.CompilerParams(
            collective_id=0, has_side_effects=True, vmem_limit_bytes=56 * 1024 * 1024
        ),
        cost_estimate=pl.CostEstimate(flops=8 * 10**9, bytes_accessed=4 * 10**6, transcendentals=10**6),
    )(
        query_nope, query_rope, latent_cache.T, up_keys, up_values, out_grad,
        response_mask.reshape(1, ROWS), boundary,
    )
    order = (3, 0, 1, 2, 4, 5)
    handed = pl.pallas_call(
        hand_over,
        out_shape=(jax.ShapeDtypeStruct((CACHE, ROWS), F32),)
        + tuple(jax.ShapeDtypeStruct(results[i].shape, results[i].dtype) for i in order[1:]),
        in_specs=[vmem] * 6,
        out_specs=(vmem,) * 6,
    )(*[results[i] for i in order])
    return (handed[1], handed[2], handed[3], handed[0].T, handed[4], handed[5])


def solution(mesh):
    in_specs = (
        P("ctx", "tp"),
        P("ctx", "tp"),
        P("ctx", None),
        P(None, "tp"),
        P(None, "tp"),
        P("ctx", "tp"),
        P("ctx"),
        P(),
    )
    out_specs = (
        P("ctx", "tp"),
        P("ctx", "tp"),
        P("ctx", "tp"),
        P("ctx", None),
        P("ctx", "tp"),
        P("ctx", "tp"),
    )
    return jax.shard_map(
        per_device, mesh=mesh, in_specs=in_specs, out_specs=out_specs, check_vma=False
    )
```
